512 devices in a mesh: dp: 2 (over z_hi), tensor: 8 (over y, core), context: 32 (over x, z_lo).
Axes of the slice: x: 4, y: 4, z: 16 (z_hi: 2, z_lo: 8; z = z_hi * 8 + z_lo), core: 2. Of those that a mesh axis runs over, the one named last changes fastest.
Arguments:
- pregate: bfloat16 [2, 256, 16384], P('dp', 'tensor', 'context'), may hold values from -6 to 6
- gate: bfloat16 [2, 256, 16384], P('dp', 'tensor', 'context'), may hold values from -6 to 6
- upstream: bfloat16 [2, 256, 16384], P('dp', 'tensor', 'context'), may hold values from -6 to 6
- filter_taps: float32 [32, 512], P(None, 'context'), may hold values from -0.046875 to 0.046875
Outputs:
- output: bfloat16 [2, 256, 16384], P('dp', 'tensor', 'context')
- grad_gate: bfloat16 [2, 256, 16384], P('dp', 'tensor', 'context')
- grad_pregate: bfloat16 [2, 256, 16384], P('dp', 'tensor', 'context')
- grad_filter: float32 [32, 512], P(None, 'context')
The draws below stay inside these ranges and needn't reach their ends.
All inputs are finite; a program needn't handle non-finite values.
Results may differ from the reference program's by a relative error of at most 0.0061.
Values may be sent and summed in bfloat16 or wider, within the bound.
A program may use at most 64 MiB of HBM per device.

```python
import math
import jax
import jax.numpy as jnp
from jax import lax

CH = 256
COLS = 512
SEQ = 16384
BATCH = 2


def level_of(rng, extent, split, smallest, top_value):
    factor_of = 1.0
    for dim, shards_of in split:
        heights = jax.random.uniform(jax.random.fold_in(jax.random.fold_in(rng, 6), dim), (shards_of,), jnp.float32, smallest / len(split), top_value / len(split))
        factor_of = factor_of * jnp.repeat(jnp.exp(heights), extent[dim] // shards_of).reshape((-1,) + (1,) * (len(extent) - 1 - dim))
    return factor_of


def gaussian(key, shape, scale, bound, cuts=(), kind=jnp.bfloat16):
    drawn = jax.random.normal(key, shape, jnp.float32) * scale
    if len(cuts) > 0:
        drawn = level_of(key, shape, cuts, -0.22, 0.18) * drawn
    return jnp.clip(drawn, min=-bound, max=bound).astype(kind)


def setup_inputs(seed: int = 0) -> dict:
    splits = jax.random.split(jax.random.key(seed), 5)
    pregate = gaussian(splits[0], (BATCH, CH, SEQ), 1.0, 6.0, ((0, 2), (1, 8), (2, 32)))
    gate = gaussian(splits[1], (BATCH, CH, SEQ), 1.0, 6.0, ((0, 2), (1, 8), (2, 32)))
    upstream = gaussian(splits[2], (BATCH, CH, SEQ), 1.0, 6.0, ((0, 2), (1, 8), (2, 32)))
    filter_taps = gaussian(splits[3], (SEQ // COLS, COLS), SEQ ** -0.5, 0.046875, ((1, 32),), jnp.float32)
    return dict(pregate=pregate, gate=gate, upstream=upstream, filter_taps=filter_taps)


def rounded(value):
    return lax.optimization_barrier(value.astype(jnp.bfloat16)).astype(jnp.float32)

def twiddles(direction):
    grid_rows = 2 * SEQ // COLS
    frequency = jnp.arange(grid_rows, dtype=jnp.int32)[:, None]
    column = jnp.arange(COLS, dtype=jnp.int32)[None, :]
    angle = (frequency * column % (2 * SEQ)).astype(jnp.float32) * (2.0 * math.pi / (2 * SEQ))
    return jnp.cos(angle) + 1j * (direction * jnp.sin(angle))

def transform(signal):
    grid_rows = 2 * SEQ // COLS
    leading = signal.shape[:-1]
    padded = jnp.concatenate([signal, jnp.zeros_like(signal)], axis=-1).reshape(leading + (grid_rows, COLS))
    half_done = jnp.fft.fft(padded, axis=-2) * twiddles(-1.0)
    half_done = rounded(half_done.real) + 1j * rounded(half_done.imag)
    return jnp.fft.fft(half_done, axis=-1)

def invert(spectrum, narrow):
    grid_rows = 2 * SEQ // COLS
    partway = jnp.fft.ifft(spectrum, axis=-1) * COLS
    if narrow:
        partway = rounded(partway.real) + 1j * rounded(partway.imag)
    turned = jnp.fft.ifft(partway * twiddles(1.0), axis=-2) * grid_rows
    leading = spectrum.shape[:-2]
    return turned[..., :SEQ // COLS, :].real.reshape(leading + (SEQ,)) / (2 * SEQ)

def reference(pregate, gate, upstream, filter_taps):
    grid_rows = 2 * SEQ // COLS
    filt = filter_taps.reshape(SEQ).astype(jnp.float32)
    filt_spec = transform(filt)

    def per_channel(carry, items):
        pre_row, gate_row, up_row = items
        pre_spec = transform(pre_row.astype(jnp.float32))
        conv = invert(pre_spec * filt_spec, True).astype(jnp.bfloat16)
        conv_f = conv.astype(jnp.float32)
        gate_f = gate_row.astype(jnp.float32)
        up_f = up_row.astype(jnp.float32)
        output = (gate_f * conv_f).astype(jnp.bfloat16)
        grad_gate = (up_f * conv_f).astype(jnp.bfloat16)
        dconv = (up_f * gate_f).astype(jnp.bfloat16)
        dconv_spec = transform(dconv.astype(jnp.float32))
        grad_pre = invert(jnp.conj(filt_spec) * dconv_spec, True).astype(jnp.bfloat16)
        cross = lax.optimization_barrier(jnp.sum(jnp.conj(pre_spec) * dconv_spec, axis=0))
        return ((carry[0] + cross.real, carry[1] + cross.imag), (output, grad_gate, grad_pre))
    start = (jnp.zeros((grid_rows, COLS), jnp.float32), jnp.zeros((grid_rows, COLS), jnp.float32))
    inputs = (jnp.swapaxes(pregate, 0, 1), jnp.swapaxes(gate, 0, 1), jnp.swapaxes(upstream, 0, 1))
    cross_sum, stacked = lax.scan(per_channel, start, inputs)
    dfilt = invert(cross_sum[0] + 1j * cross_sum[1], False)
    norm_factor = 1.0 / math.sqrt(CH * BATCH * SEQ)
    grad_filter = (dfilt * norm_factor).reshape(SEQ // COLS, COLS)
    output = jnp.swapaxes(stacked[0], 0, 1)
    grad_gate = jnp.swapaxes(stacked[1], 0, 1)
    grad_pregate = jnp.swapaxes(stacked[2], 0, 1)
    return (output, grad_gate, grad_pregate, grad_filter)
```

```python
import math

import jax
import jax.numpy as jnp
import ml_dtypes
import numpy as np
from jax import lax
from jax.experimental import pallas as pl
from jax.experimental.pallas import tpu as pltpu
from jax.sharding import PartitionSpec as P


COLS = 512
ROWS = 32
POINTS = ROWS * COLS
LANES = 128
QUADS = COLS // LANES
F32 = jnp.float32
BF16 = jnp.bfloat16
MESH = pl.DeviceIdType.MESH


def split(table):
    high = table.astype(ml_dtypes.bfloat16)
    low = (table - high.astype(np.float64)).astype(ml_dtypes.bfloat16)
    return high, low


def make_tables(norm):
    r = np.arange(ROWS)
    k1 = np.arange(ROWS)
    c = np.arange(COLS)
    inner = 2.0 * np.pi * (np.outer(c, c) % COLS) / COLS
    wave = np.concatenate([np.cos(inner), np.sin(inner)], axis=1)
    wave = np.stack(split(wave))
    phase = 2.0 * np.pi * (np.outer(4 * k1 + 1, c) % (4 * POINTS)) / (4 * POINTS)
    twist = np.stack([np.cos(phase), np.sin(phase)]).astype(np.float32)
    turned = np.concatenate([np.cos(phase.T)] * 2 + [np.sin(phase.T)] * 2, axis=1).astype(np.float32)
    outer = 2.0 * np.pi * (np.outer(4 * k1 + 1, r) % (4 * ROWS)) / (4 * ROWS)
    first = np.concatenate([np.cos(outer), -np.sin(outer)], axis=0)
    first_high, first_low = split(first)
    analyse = np.concatenate([first_high, first_low], axis=1)
    analyse_taps = np.concatenate(
        [np.concatenate([first_high] * 4, axis=1), np.concatenate([first_low] * 4, axis=1)], axis=0
    )
    last_high, last_low = split(first.T / POINTS)
    build = np.concatenate([last_high, last_low], axis=1)
    wide = np.concatenate([first * (norm / POINTS)] * 2, axis=0)
    wide = np.concatenate([wide] * 4, axis=1)
    build_taps = np.concatenate(split(wide), axis=0)
    small = np.zeros((5, 256, LANES), ml_dtypes.bfloat16)
    small[0, :64, :64] = analyse
    small[1, :128] = analyse_taps
    small[2, :32] = build
    small[3, :256] = build_taps
    return wave, twist, turned, small[:4]


def mm(a, b):
    return jnp.dot(a, b, preferred_element_type=F32)


def mm_nt(a, b):
    return lax.dot_general(a, b, (((1,), (1,)), ((), ())), preferred_element_type=F32)


def kernel(
    pre_hbm, gate_hbm, up_hbm, taps_hbm, wave_hbm, twist_hbm, turned_hbm, small_hbm,
    out_ref, gg_ref, gp_ref, gf_ref,
    pre_v, gate_v, up_v, taps_v, wave_v, twist_v, turned_v, small_v, pack_v,
    main_s, main_r, taps_s, taps_r, back_s, back_r, part_s, part_r, sum_s, sum_r,
    in_sem, table_sem, send_sem, recv_sem,
):
    dp = lax.axis_index("dp")
    tensor = lax.axis_index("tensor")
    me = lax.axis_index("context")
    n_tensor = lax.axis_size("tensor")
    n_rep = lax.axis_size("dp") * n_tensor
    rep = dp * n_tensor + tensor

    barrier = pltpu.get_barrier_semaphore()

    def row_peer(step):
        return (dp, tensor, lax.rem(me + step, ROWS))

    def rep_peer(step):
        other = lax.rem(rep + step, n_rep)
        return (other // n_tensor, lax.rem(other, n_tensor), me)

    def greet_row(step, carry):
        pl.semaphore_signal(barrier, inc=1, device_id=row_peer(step), device_id_type=MESH)
        return carry

    def greet_rep(step, carry):
        pl.semaphore_signal(barrier, inc=1, device_id=rep_peer(step), device_id_type=MESH)
        return carry

    lax.fori_loop(1, ROWS, greet_row, 0)
    lax.fori_loop(1, n_rep, greet_rep, 0)

    loads = [
        pltpu.make_async_copy(src, dst, in_sem.at[n])
        for n, (src, dst) in enumerate(
            [(pre_hbm, pre_v), (gate_hbm, gate_v), (up_hbm, up_v), (taps_hbm, taps_v)]
        )
    ]
    tables = [
        pltpu.make_async_copy(src, dst, table_sem.at[n])
        for n, (src, dst) in enumerate(
            [(small_hbm, small_v), (twist_hbm, twist_v), (wave_hbm, wave_v), (turned_hbm, turned_v)]
        )
    ]
    for copy in loads:
        copy.start()
    for copy in tables:
        copy.start()
    for copy in loads:
        copy.wait()

    gate = gate_v[...].astype(F32)
    up = up_v[...].astype(F32)
    dconv = (up * gate).astype(BF16).astype(F32)
    pre = pre_v[...].astype(F32)
    for p, signal in enumerate((pre, dconv)):
        for q in range(QUADS):
            pack_v[pl.ds(p * QUADS + q, ROWS, stride=8), :] = signal[:, q * LANES:(q + 1) * LANES]
    main_s[...] = pack_v[...].reshape(ROWS, 8, LANES).astype(BF16)

    taps = taps_v[...]
    taps_high = taps.astype(BF16).astype(F32)
    taps_low = taps - taps_high
    stacked = jnp.concatenate([taps_high, taps_low, taps_high, taps_low], axis=0)
    row = lax.broadcasted_iota(jnp.int32, (LANES, 16), 0)
    lane = lax.broadcasted_iota(jnp.int32, (LANES, 16), 1)
    stacked = jnp.where((row < 64) == (lane < 8), stacked, 0.0).astype(BF16)
    fold_row = lax.broadcasted_iota(jnp.int32, (16, 16), 0)
    fold_lane = lax.broadcasted_iota(jnp.int32, (16, 16), 1)
    fold = jnp.where((fold_row == fold_lane) | (fold_row + 8 == fold_lane), 1.0, 0.0).astype(BF16)
    taps_s[...] = mm_nt(fold, stacked)[:8].astype(BF16)

    pl.semaphore_wait(barrier, ROWS - 1 + n_rep - 1)

    def exchange(source, target, phase, peers, count, mine):
        def send(step, carry):
            pltpu.make_async_remote_copy(
                src_ref=source(step),
                dst_ref=target.at[mine],
                send_sem=send_sem.at[phase],
                recv_sem=recv_sem.at[phase],
                device_id=peers(step),
                device_id_type=MESH,
            ).start()
            return carry

        lax.fori_loop(1, count, send, 0)
        pltpu.make_async_copy(source(0), target.at[mine], recv_sem.at[phase]).start()

    def arrive(target, phase):
        pltpu.make_async_copy(target, target, recv_sem.at[phase]).wait()

    def left(target, phase, count):
        part = target.at[pl.ds(0, count - 1)]
        pltpu.make_async_copy(part, part, send_sem.at[phase]).wait()

    exchange(lambda s: main_s.at[lax.rem(me + s, ROWS)], main_r, 0, row_peer, ROWS, me)
    exchange(lambda s: taps_s, taps_r, 1, row_peer, ROWS, me)

    for copy in tables:
        copy.wait()
    cos = twist_v[0]
    sin = twist_v[1]

    def forward_twist(re, im):
        return (re * cos + im * sin).astype(BF16), (im * cos - re * sin).astype(BF16)

    def inverse_twist(re, im):
        return (re * cos - im * sin).astype(BF16), (re * sin + im * cos).astype(BF16)

    arrive(main_r, 0)
    pack_v[...] = main_r[...].astype(F32).reshape(ROWS * 8, LANES)
    analyse = small_v[0, :64, :64]
    halves = []
    for p in range(2):
        rows = [pack_v[pl.ds(p * QUADS + q, ROWS, stride=8), :] for q in range(QUADS)]
        grid = jnp.concatenate(rows, axis=1).astype(BF16)
        part = mm(analyse, jnp.concatenate([grid, grid], axis=0))
        halves.extend(forward_twist(part[:32], part[32:]))
    lhs = jnp.concatenate(halves, axis=0)
    wide = mm(lhs, wave_v[0]) + mm(lhs, wave_v[1])

    def spectrum(base):
        re_c, re_s = wide[base:base + 32, :COLS], wide[base:base + 32, COLS:]
        im_c, im_s = wide[base + 32:base + 64, :COLS], wide[base + 32:base + 64, COLS:]
        return re_c + im_s, im_c - re_s

    pre_re, pre_im = spectrum(0)
    dc_re, dc_im = spectrum(64)

    x_re = pre_re * dc_re + pre_im * dc_im
    x_im = pre_re * dc_im - pre_im * dc_re
    x_re, x_im = x_re.astype(BF16), x_im.astype(BF16)
    up_row = jnp.concatenate([x_re, -x_im], axis=1)
    mid_row = jnp.concatenate([x_im, x_re], axis=1)
    low_row = jnp.concatenate([-x_im, -x_re], axis=1)
    rhs = jnp.concatenate([up_row, mid_row, low_row, up_row], axis=0)
    back = mm_nt(wave_v[0], rhs) + mm_nt(wave_v[1], rhs)
    back = (back * turned_v[...]).astype(BF16)
    share = mm(jnp.concatenate([back, back], axis=1), small_v[3])
    share = share.reshape(ROWS, 2, 8, LANES)
    lane = lax.broadcasted_iota(jnp.int32, (ROWS, 8, LANES), 2)
    share = jnp.where(lane < 64, share[:, 0], share[:, 1])
    share_high = share.astype(BF16).astype(F32)
    share = jnp.where(lax.rem(lane, 64) < 32, share_high, share - share_high)
    part_s[...] = share.astype(BF16)
    exchange(lambda s: part_s.at[lax.rem(me + s, ROWS)], part_r, 2, row_peer, ROWS, me)

    arrive(taps_r, 1)
    taps = taps_r[...].astype(F32)
    taps = jnp.stack([jnp.where(lane < 64, taps, 0.0), jnp.where(lane < 64, 0.0, taps)], axis=1)
    taps = taps.reshape(COLS, LANES).astype(BF16)
    part = mm_nt(small_v[1, :64], taps) + mm_nt(small_v[1, 64:128], taps)
    lhs = jnp.concatenate(forward_twist(part[:32], part[32:]), axis=0)
    wide = mm(lhs, wave_v[0]) + mm(lhs, wave_v[1])
    f_re, f_im = spectrum(0)

    products = [
        pre_re * f_re - pre_im * f_im,
        pre_re * f_im + pre_im * f_re,
        f_re * dc_re + f_im * dc_im,
        f_re * dc_im - f_im * dc_re,
    ]
    lhs = jnp.concatenate([product.astype(BF16) for product in products], axis=0)
    wide = mm(lhs, wave_v[0]) + mm(lhs, wave_v[1])
    build = small_v[2, :32]
    for p in range(2):
        base = 64 * p
        re_c, re_s = wide[base:base + 32, :COLS], wide[base:base + 32, COLS:]
        im_c, im_s = wide[base + 32:base + 64, :COLS], wide[base + 32:base + 64, COLS:]
        half = jnp.concatenate(inverse_twist(re_c - im_s, re_s + im_c), axis=0)
        result = mm(build, jnp.concatenate([half, half], axis=0))
        for q in range(QUADS):
            pack_v[pl.ds(p * QUADS + q, ROWS, stride=8), :] = result[:, q * LANES:(q + 1) * LANES]
    back_s[...] = pack_v[...].reshape(ROWS, 8, LANES).astype(BF16)
    exchange(lambda s: back_s.at[lax.rem(me + s, ROWS)], back_r, 3, row_peer, ROWS, me)

    arrive(part_r, 2)
    sum_s[...] = jnp.sum(part_r[...].astype(F32), axis=0)
    exchange(lambda s: sum_s, sum_r, 4, rep_peer, n_rep, rep)

    arrive(back_r, 3)
    pack_v[...] = back_r[...].astype(F32).reshape(ROWS * 8, LANES)
    rows = [pack_v[pl.ds(n, ROWS, stride=8), :] for n in range(8)]
    conv = jnp.concatenate(rows[:QUADS], axis=1)
    out_ref[...] = (gate * conv).astype(BF16)
    gg_ref[...] = (up * conv).astype(BF16)
    gp_ref[...] = jnp.concatenate(rows[QUADS:], axis=1).astype(BF16)

    arrive(sum_r, 4)
    total = jnp.sum(sum_r[...], axis=0)
    total = total + pltpu.roll(total, 96, 1)
    total = jnp.transpose(total)
    gf_ref[:, 0:8] = total[0:32]
    gf_ref[:, 8:16] = total[64:96]

    left(main_r, 0, ROWS)
    left(taps_r, 1, ROWS)
    left(part_r, 2, ROWS)
    left(back_r, 3, ROWS)
    left(sum_r, 4, n_rep)


def solution(mesh):
    n_rep = mesh.shape["dp"] * mesh.shape["tensor"]
    norm = 1.0 / math.sqrt(n_rep * mesh.shape["context"] * POINTS)
    wave, twist, turned, small = make_tables(norm)

    def body(pregate, gate, upstream, filter_taps):
        block = jax.ShapeDtypeStruct((ROWS, COLS), BF16)
        message = pltpu.VMEM((ROWS, 8, LANES), BF16)
        results = pl.pallas_call(
            kernel,
            out_shape=[block, block, block, jax.ShapeDtypeStruct((ROWS, 16), F32)],
            in_specs=[pl.BlockSpec(memory_space=pl.ANY)] * 8,
            out_specs=[pl.BlockSpec(memory_space=pltpu.VMEM)] * 4,
            scratch_shapes=[
                pltpu.VMEM((ROWS, COLS), BF16),
                pltpu.VMEM((ROWS, COLS), BF16),
                pltpu.VMEM((ROWS, COLS), BF16),
                pltpu.VMEM((ROWS, 16), F32),
                pltpu.VMEM(wave.shape, BF16),
                pltpu.VMEM(twist.shape, F32),
                pltpu.VMEM(turned.shape, F32),
                pltpu.VMEM(small.shape, BF16),
                pltpu.VMEM((ROWS * 8, LANES), F32),
                message,
                message,
                pltpu.VMEM((8, LANES), BF16),
                message,
                message,
                message,
                message,
                message,
                pltpu.VMEM((8, LANES), F32),
                pltpu.VMEM((n_rep, 8, LANES), F32),
                pltpu.SemaphoreType.DMA((4,)),
                pltpu.SemaphoreType.DMA((4,)),
                pltpu.SemaphoreType.DMA((5,)),
                pltpu.SemaphoreType.DMA((5,)),
            ],
            compiler_params=pltpu.CompilerParams(
                collective_id=0, has_side_effects=True, vmem_limit_bytes=40 * 1024 * 1024
            ),
        )(
            pregate.reshape(ROWS, COLS),
            gate.reshape(ROWS, COLS),
            upstream.reshape(ROWS, COLS),
            filter_taps,
            jnp.asarray(wave),
            jnp.asarray(twist),
            jnp.asarray(turned),
            jnp.asarray(small),
        )
        shape = pregate.shape
        return tuple(value.reshape(shape) for value in results[:3]) + (results[3],)

    whole = P("dp", "tensor", "context")
    specs = (whole, whole, whole, P(None, "context"))
    return jax.shard_map(body, mesh=mesh, in_specs=specs, out_specs=specs, check_vma=False)
```

```python
import math

import jax
import jax.numpy as jnp
import ml_dtypes
import numpy as np
from jax import lax
from jax.experimental import pallas as pl
from jax.experimental.pallas import tpu as pltpu
from jax.sharding import PartitionSpec as P


COLS = 512
ROWS = 32
POINTS = ROWS * COLS
LANES = 128
QUADS = COLS // LANES
F32 = jnp.float32
BF16 = jnp.bfloat16
MESH = pl.DeviceIdType.MESH


def split(table):
    high = table.astype(ml_dtypes.bfloat16)
    low = (table - high.astype(np.float64)).astype(ml_dtypes.bfloat16)
    return high, low


def make_tables(norm):
    r = np.arange(ROWS)
    k1 = np.arange(ROWS)
    c = np.arange(COLS)
    inner = 2.0 * np.pi * (np.outer(c, c) % COLS) / COLS
    wave = np.concatenate([np.cos(inner), np.sin(inner)], axis=1)
    wave = np.concatenate(split(wave), axis=0)
    wave = np.stack(np.split(wave, 2 * QUADS, axis=1))
    phase = 2.0 * np.pi * (np.outer(4 * k1 + 1, c) % (4 * POINTS)) / (4 * POINTS)
    twist = np.stack([np.cos(phase), np.sin(phase)]).astype(np.float32)
    turned = np.concatenate([np.cos(phase.T)] * 2 + [np.sin(phase.T)] * 2, axis=1).astype(np.float32)
    outer = 2.0 * np.pi * (np.outer(4 * k1 + 1, r) % (4 * ROWS)) / (4 * ROWS)
    first = np.concatenate([np.cos(outer), -np.sin(outer)], axis=0)
    first_high, first_low = split(first)
    analyse = np.concatenate([first_high, first_low], axis=1)
    analyse_taps = np.concatenate(
        [np.concatenate([first_high] * 4, axis=1), np.concatenate([first_low] * 4, axis=1)], axis=0
    )
    last_high, last_low = split(first.T / POINTS)
    build = np.concatenate([last_high, last_low], axis=1)
    wide = np.concatenate([first * (norm / POINTS)] * 2, axis=0)
    wide = np.concatenate([wide] * 4, axis=1)
    build_taps = np.concatenate(split(wide), axis=0)
    small = np.zeros((5, 256, LANES), ml_dtypes.bfloat16)
    small[0, :64, :64] = analyse
    small[1, :128] = analyse_taps
    small[2, :32] = build
    small[3, :256] = build_taps
    return wave, twist, turned, small[:4]


def mm(a, b):
    return jnp.dot(a, b, preferred_element_type=F32)


def mm_nt(a, b):
    return lax.dot_general(a, b, (((1,), (1,)), ((), ())), preferred_element_type=F32)


def kernel(
    pre_hbm, gate_hbm, up_hbm, taps_hbm, wave_hbm, twist_hbm, turned_hbm, small_hbm,
    out_ref, gg_ref, gp_ref, gf_ref,
    pre_v, gate_v, up_v, taps_v, wave_v, twist_v, turned_v, small_v, pack_v,
    main_s, main_r, taps_s, taps_r, back_s, back_r, part_s, part_r, sum_s, sum_r,
    in_sem, table_sem, send_sem, recv_sem,
):
    dp = lax.axis_index("dp")
    tensor = lax.axis_index("tensor")
    me = lax.axis_index("context")
    n_tensor = lax.axis_size("tensor")
    n_rep = lax.axis_size("dp") * n_tensor
    rep = dp * n_tensor + tensor

    barrier = pltpu.get_barrier_semaphore()

    def row_peer(step):
        return (dp, tensor, lax.rem(me + step, ROWS))

    def rep_peer(step):
        other = lax.rem(rep + step, n_rep)
        return (other // n_tensor, lax.rem(other, n_tensor), me)

    def greet_row(step, carry):
        pl.semaphore_signal(barrier, inc=1, device_id=row_peer(step), device_id_type=MESH)
        return carry

    def greet_rep(step, carry):
        pl.semaphore_signal(barrier, inc=1, device_id=rep_peer(step), device_id_type=MESH)
        return carry

    lax.fori_loop(1, ROWS, greet_row, 0)
    lax.fori_loop(1, n_rep, greet_rep, 0)

    loads = [
        pltpu.make_async_copy(src, dst, in_sem.at[n])
        for n, (src, dst) in enumerate(
            [(pre_hbm, pre_v), (gate_hbm, gate_v), (up_hbm, up_v), (taps_hbm, taps_v)]
        )
    ]
    tables = [
        pltpu.make_async_copy(src, dst, table_sem.at[n])
        for n, (src, dst) in enumerate(
            [(small_hbm, small_v), (twist_hbm, twist_v), (wave_hbm, wave_v), (turned_hbm, turned_v)]
        )
    ]
    for copy in loads:
        copy.start()
    for copy in tables:
        copy.start()
    for copy in loads:
        copy.wait()

    gate = gate_v[...].astype(F32)
    up = up_v[...].astype(F32)
    dconv = (up * gate).astype(BF16).astype(F32)
    pre = pre_v[...].astype(F32)
    for p, signal in enumerate((pre, dconv)):
        for q in range(QUADS):
            pack_v[pl.ds(p * QUADS + q, ROWS, stride=8), :] = signal[:, q * LANES:(q + 1) * LANES]
    main_s[...] = pack_v[...].reshape(ROWS, 8, LANES).astype(BF16)

    taps = taps_v[...]
    taps_high = taps.astype(BF16).astype(F32)
    taps_low = taps - taps_high
    taps_s[...] = jnp.concatenate(
        [taps_high[:8], taps_low[:8], taps_high[8:], taps_low[8:]], axis=1
    ).astype(BF16)

    pl.semaphore_wait(barrier, ROWS - 1 + n_rep - 1)

    def exchange(source, target, phase, peers, count, mine):
        def send(step, carry):
            pltpu.make_async_remote_copy(
                src_ref=source(step),
                dst_ref=target.at[mine],
                send_sem=send_sem.at[phase],
                recv_sem=recv_sem.at[phase],
                device_id=peers(step),
                device_id_type=MESH,
            ).start()
            return carry

        lax.fori_loop(1, count, send, 0)
        pltpu.make_async_copy(source(0), target.at[mine], recv_sem.at[phase]).start()

    def arrive(target, phase):
        pltpu.make_async_copy(target, target, recv_sem.at[phase]).wait()

    def left(target, phase, count):
        part = target.at[pl.ds(0, count - 1)]
        pltpu.make_async_copy(part, part, send_sem.at[phase]).wait()

    exchange(lambda s: main_s.at[lax.rem(me + s, ROWS)], main_r, 0, row_peer, ROWS, me)
    exchange(lambda s: taps_s, taps_r, 1, row_peer, ROWS, me)

    for copy in tables:
        copy.wait()
    wave_high = jnp.concatenate([wave_v[n, :COLS] for n in range(2 * QUADS)], axis=1)
    wave_low = jnp.concatenate([wave_v[n, COLS:] for n in range(2 * QUADS)], axis=1)
    cos = twist_v[0]
    sin = twist_v[1]

    def forward_twist(re, im):
        return (re * cos + im * sin).astype(BF16), (im * cos - re * sin).astype(BF16)

    def inverse_twist(re, im):
        return (re * cos - im * sin).astype(BF16), (re * sin + im * cos).astype(BF16)

    arrive(main_r, 0)
    pack_v[...] = main_r[...].astype(F32).reshape(ROWS * 8, LANES)
    analyse = small_v[0, :64, :64]
    halves = []
    for p in range(2):
        rows = [pack_v[pl.ds(p * QUADS + q, ROWS, stride=8), :] for q in range(QUADS)]
        grid = jnp.concatenate(rows, axis=1).astype(BF16)
        part = mm(analyse, jnp.concatenate([grid, grid], axis=0))
        halves.extend(forward_twist(part[:32], part[32:]))
    lhs = jnp.concatenate(halves, axis=0)
    wide = mm(lhs, wave_high) + mm(lhs, wave_low)

    def spectrum(base):
        re_c, re_s = wide[base:base + 32, :COLS], wide[base:base + 32, COLS:]
        im_c, im_s = wide[base + 32:base + 64, :COLS], wide[base + 32:base + 64, COLS:]
        return re_c + im_s, im_c - re_s

    pre_re, pre_im = spectrum(0)
    dc_re, dc_im = spectrum(64)

    x_re = pre_re * dc_re + pre_im * dc_im
    x_im = pre_re * dc_im - pre_im * dc_re
    x_re, x_im = x_re.astype(BF16), x_im.astype(BF16)
    up_row = jnp.concatenate([x_re, -x_im], axis=1)
    mid_row = jnp.concatenate([x_im, x_re], axis=1)
    low_row = jnp.concatenate([-x_im, -x_re], axis=1)
    rhs = jnp.concatenate([up_row, mid_row, low_row, up_row], axis=0)
    back = mm_nt(wave_high, rhs) + mm_nt(wave_low, rhs)
    back = (back * turned_v[...]).astype(BF16)
    share = mm(jnp.concatenate([back, back], axis=1), small_v[3])
    share = share.reshape(ROWS, 2, 8, LANES)
    lane = lax.broadcasted_iota(jnp.int32, (ROWS, 8, LANES), 2)
    share = jnp.where(lane < 64, share[:, 0], share[:, 1])
    share_high = share.astype(BF16).astype(F32)
    share = jnp.where(lax.rem(lane, 64) < 32, share_high, share - share_high)
    part_s[...] = share.astype(BF16)
    exchange(lambda s: part_s.at[lax.rem(me + s, ROWS)], part_r, 2, row_peer, ROWS, me)

    arrive(taps_r, 1)
    taps = taps_r[...].astype(F32)
    taps = jnp.stack([jnp.where(lane < 64, taps, 0.0), jnp.where(lane < 64, 0.0, taps)], axis=1)
    taps = taps.reshape(COLS, LANES).astype(BF16)
    part = mm_nt(small_v[1, :64], taps) + mm_nt(small_v[1, 64:128], taps)
    lhs = jnp.concatenate(forward_twist(part[:32], part[32:]), axis=0)
    wide = mm(lhs, wave_high) + mm(lhs, wave_low)
    f_re, f_im = spectrum(0)

    products = [
        pre_re * f_re - pre_im * f_im,
        pre_re * f_im + pre_im * f_re,
        f_re * dc_re + f_im * dc_im,
        f_re * dc_im - f_im * dc_re,
    ]
    lhs = jnp.concatenate([product.astype(BF16) for product in products], axis=0)
    wide = mm(lhs, wave_high) + mm(lhs, wave_low)
    build = small_v[2, :32]
    for p in range(2):
        base = 64 * p
        re_c, re_s = wide[base:base + 32, :COLS], wide[base:base + 32, COLS:]
        im_c, im_s = wide[base + 32:base + 64, :COLS], wide[base + 32:base + 64, COLS:]
        half = jnp.concatenate(inverse_twist(re_c - im_s, re_s + im_c), axis=0)
        result = mm(build, jnp.concatenate([half, half], axis=0))
        for q in range(QUADS):
            pack_v[pl.ds(p * QUADS + q, ROWS, stride=8), :] = result[:, q * LANES:(q + 1) * LANES]
    back_s[...] = pack_v[...].reshape(ROWS, 8, LANES).astype(BF16)
    exchange(lambda s: back_s.at[lax.rem(me + s, ROWS)], back_r, 3, row_peer, ROWS, me)

    arrive(part_r, 2)
    sum_s[...] = jnp.sum(part_r[...].astype(F32), axis=0)
    exchange(lambda s: sum_s, sum_r, 4, rep_peer, n_rep, rep)

    arrive(back_r, 3)
    pack_v[...] = back_r[...].astype(F32).reshape(ROWS * 8, LANES)
    rows = [pack_v[pl.ds(n, ROWS, stride=8), :] for n in range(8)]
    conv = jnp.concatenate(rows[:QUADS], axis=1)
    out_ref[...] = (gate * conv).astype(BF16)
    gg_ref[...] = (up * conv).astype(BF16)
    gp_ref[...] = jnp.concatenate(rows[QUADS:], axis=1).astype(BF16)

    arrive(sum_r, 4)
    total = jnp.sum(sum_r[...], axis=0)
    total = total + pltpu.roll(total, 96, 1)
    gf_ref[0:8, :] = total[:, 0:32]
    gf_ref[8:16, :] = total[:, 64:96]

    left(main_r, 0, ROWS)
    left(taps_r, 1, ROWS)
    left(part_r, 2, ROWS)
    left(back_r, 3, ROWS)
    left(sum_r, 4, n_rep)


def solution(mesh):
    n_rep = mesh.shape["dp"] * mesh.shape["tensor"]
    norm = 1.0 / math.sqrt(n_rep * mesh.shape["context"] * POINTS)
    wave, twist, turned, small = make_tables(norm)

    def body(pregate, gate, upstream, filter_taps):
        block = jax.ShapeDtypeStruct((ROWS, COLS), BF16)
        message = pltpu.VMEM((ROWS, 8, LANES), BF16)
        results = pl.pallas_call(
            kernel,
            out_shape=[block, block, block, jax.ShapeDtypeStruct((16, ROWS), F32)],
            in_specs=[pl.BlockSpec(memory_space=pltpu.HBM)] * 8,
            out_specs=[pl.BlockSpec(memory_space=pltpu.VMEM)] * 4,
            scratch_shapes=[
                pltpu.VMEM((ROWS, COLS), BF16),
                pltpu.VMEM((ROWS, COLS), BF16),
                pltpu.VMEM((ROWS, COLS), BF16),
                pltpu.VMEM((16, ROWS), F32),
                pltpu.VMEM(wave.shape, BF16),
                pltpu.VMEM(twist.shape, F32),
                pltpu.VMEM(turned.shape, F32),
                pltpu.VMEM(small.shape, BF16),
                pltpu.VMEM((ROWS * 8, LANES), F32),
                message,
                message,
                pltpu.VMEM((8, LANES), BF16),
                message,
                message,
                message,
                message,
                message,
                pltpu.VMEM((8, LANES), F32),
                pltpu.VMEM((n_rep, 8, LANES), F32),
                pltpu.SemaphoreType.DMA((4,)),
                pltpu.SemaphoreType.DMA((4,)),
                pltpu.SemaphoreType.DMA((5,)),
                pltpu.SemaphoreType.DMA((5,)),
            ],
            compiler_params=pltpu.CompilerParams(
                collective_id=0, has_side_effects=True, vmem_limit_bytes=56 * 1024 * 1024
            ),
        )(
            pregate.reshape(ROWS, COLS),
            gate.reshape(ROWS, COLS),
            upstream.reshape(ROWS, COLS),
            filter_taps.T,
            jnp.asarray(wave),
            jnp.asarray(twist),
            jnp.asarray(turned),
            jnp.asarray(small),
        )
        shape = pregate.shape
        return tuple(value.reshape(shape) for value in results[:3]) + (results[3].T,)

    whole = P("dp", "tensor", "context")
    specs = (whole, whole, whole, P(None, "context"))
    return jax.shard_map(body, mesh=mesh, in_specs=specs, out_specs=specs, check_vma=False)
```

```python
import math

import jax
import jax.numpy as jnp
import ml_dtypes
import numpy as np
from jax import lax
from jax.experimental import pallas as pl
from jax.experimental.pallas import tpu as pltpu
from jax.sharding import PartitionSpec as P


COLS = 512
ROWS = 32
POINTS = ROWS * COLS
LANES = 128
QUADS = COLS // LANES
SLABS = 8
COPIES = 2 * SLABS
F32 = jnp.float32
BF16 = jnp.bfloat16
MESH = pl.DeviceIdType.MESH


def split(table):
    high = table.astype(ml_dtypes.bfloat16)
    low = (table - high.astype(np.float64)).astype(ml_dtypes.bfloat16)
    return high, low


def make_tables(norm):
    r = np.arange(ROWS)
    k1 = np.arange(ROWS)
    c = np.arange(COLS)
    inner = 2.0 * np.pi * (np.outer(c, c) % COLS) / COLS
    wave = np.concatenate([np.cos(inner), np.sin(inner)], axis=1)
    wave = np.concatenate(split(wave), axis=0)
    wave = np.stack(np.split(wave, 2 * QUADS, axis=1))
    phase = 2.0 * np.pi * (np.outer(4 * k1 + 1, c) % (4 * POINTS)) / (4 * POINTS)
    twist = np.stack([np.cos(phase), np.sin(phase)]).astype(np.float32)
    turned = np.concatenate([np.cos(phase.T)] * 2 + [np.sin(phase.T)] * 2, axis=1).astype(np.float32)
    outer = 2.0 * np.pi * (np.outer(4 * k1 + 1, r) % (4 * ROWS)) / (4 * ROWS)
    first = np.concatenate([np.cos(outer), -np.sin(outer)], axis=0)
    first_high, first_low = split(first)
    analyse = np.concatenate([first_high, first_low], axis=1)
    analyse_taps = np.concatenate(
        [np.concatenate([first_high] * 4, axis=1), np.concatenate([first_low] * 4, axis=1)], axis=0
    )
    last_high, last_low = split(first.T / POINTS)
    build = np.concatenate([last_high, last_low], axis=1)
    wide = np.concatenate([first * (norm / POINTS)] * 2, axis=0)
    wide = np.concatenate([wide] * 4, axis=1)
    build_taps = np.concatenate(split(wide), axis=0)
    small = np.zeros((5, 256, LANES), ml_dtypes.bfloat16)
    small[0, :64, :64] = analyse
    small[1, :128] = analyse_taps
    small[2, :32] = build
    small[3, :256] = build_taps
    return wave, twist, turned, small[:4]


def mm(a, b):
    return jnp.dot(a, b, preferred_element_type=F32)


def mm_nt(a, b):
    return lax.dot_general(a, b, (((1,), (1,)), ((), ())), preferred_element_type=F32)


def pair(value):
    lane = lax.broadcasted_iota(jnp.int32, value.shape, value.ndim - 1)
    high = value.astype(BF16).astype(F32)
    return jnp.where(lax.rem(lane, 64) < 32, high, value - high).astype(BF16)


def kernel(
    pre_hbm, gate_hbm, up_hbm, taps_hbm, wave_hbm, twist_hbm, turned_hbm, small_hbm,
    out_ref, gg_ref, gp_ref, gf_ref,
    pre_v, gate_v, up_v, taps_v, wave_v, twist_v, turned_v, small_v, pack_v,
    main_s, main_r, taps_s, taps_r, back_s, back_r, part_s, part_r, sum_s, sum_r,
    in_sem, table_sem, send_sem, recv_sem,
):
    dp = lax.axis_index("dp")
    tensor = lax.axis_index("tensor")
    me = lax.axis_index("context")
    x, z = me // SLABS, lax.rem(me, SLABS)
    plane = x * SLABS + tensor

    barrier = pltpu.get_barrier_semaphore()

    def row_peer(step):
        return (dp, tensor, lax.rem(me + step, ROWS))

    def tensor_peer(step):
        return (dp, lax.rem(tensor + step, SLABS), me)

    def plane_peer(step):
        other = lax.rem(plane + step, ROWS)
        return (dp, lax.rem(other, SLABS), other // SLABS * SLABS + z)

    def owner(step):
        return (lax.rem(dp + step // SLABS, 2), lax.rem(tensor + step, SLABS), plane)

    def greet(peers):
        def signal(step, carry):
            pl.semaphore_signal(barrier, inc=1, device_id=peers(step), device_id_type=MESH)
            return carry

        return signal

    lax.fori_loop(1, ROWS, greet(row_peer), 0)
    lax.fori_loop(1, SLABS, greet(tensor_peer), 0)
    greet(lambda step: (1 - dp, tensor, me))(0, 0)

    loads = [
        pltpu.make_async_copy(src, dst, in_sem.at[n])
        for n, (src, dst) in enumerate(
            [(pre_hbm, pre_v), (gate_hbm, gate_v), (up_hbm, up_v), (taps_hbm, taps_v)]
        )
    ]
    tables = [
        pltpu.make_async_copy(src, dst, table_sem.at[n])
        for n, (src, dst) in enumerate(
            [(small_hbm, small_v), (twist_hbm, twist_v), (wave_hbm, wave_v), (turned_hbm, turned_v)]
        )
    ]
    for copy in loads:
        copy.start()
    for copy in tables:
        copy.start()
    for copy in loads:
        copy.wait()

    gate = gate_v[...].astype(F32)
    up = up_v[...].astype(F32)
    dconv = (up * gate).astype(BF16).astype(F32)
    pre = pre_v[...].astype(F32)
    for p, signal in enumerate((pre, dconv)):
        for q in range(QUADS):
            pack_v[pl.ds(p * QUADS + q, ROWS, stride=8), :] = signal[:, q * LANES:(q + 1) * LANES]
    main_s[...] = pack_v[...].reshape(ROWS, 8, LANES).astype(BF16)

    taps = taps_v[...]
    taps_high = taps.astype(BF16).astype(F32)
    taps_low = taps - taps_high
    taps_s[...] = jnp.concatenate(
        [taps_high[:8], taps_low[:8], taps_high[8:], taps_low[8:]], axis=1
    ).astype(BF16)

    pl.semaphore_wait(barrier, ROWS - 1 + SLABS - 1 + 1)

    def send(source, target, phase, peer, mine):
        pltpu.make_async_remote_copy(
            src_ref=source,
            dst_ref=target.at[mine],
            send_sem=send_sem.at[phase],
            recv_sem=recv_sem.at[phase],
            device_id=peer,
            device_id_type=MESH,
        ).start()

    def exchange(source, target, phase, peers, count, mine):
        def one(step, carry):
            send(source(step), target, phase, peers(step), mine)
            return carry

        lax.fori_loop(1, count, one, 0)

    def keep(source, target, phase, mine):
        pltpu.make_async_copy(source, target.at[mine], recv_sem.at[phase]).start()

    def arrive(target, phase):
        pltpu.make_async_copy(target, target, recv_sem.at[phase]).wait()

    def left(target, phase, count):
        part = target.at[pl.ds(0, count - 1)]
        pltpu.make_async_copy(part, part, send_sem.at[phase]).wait()

    exchange(lambda s: main_s.at[lax.rem(me + s, ROWS)], main_r, 0, row_peer, ROWS, me)
    keep(main_s.at[me], main_r, 0, me)
    exchange(lambda s: taps_s, taps_r, 1, row_peer, ROWS, me)
    keep(taps_s, taps_r, 1, me)

    for copy in tables:
        copy.wait()
    wave_high = jnp.concatenate([wave_v[n, :COLS] for n in range(2 * QUADS)], axis=1)
    wave_low = jnp.concatenate([wave_v[n, COLS:] for n in range(2 * QUADS)], axis=1)
    cos = twist_v[0]
    sin = twist_v[1]

    def forward_twist(re, im):
        return (re * cos + im * sin).astype(BF16), (im * cos - re * sin).astype(BF16)

    def inverse_twist(re, im):
        return (re * cos - im * sin).astype(BF16), (re * sin + im * cos).astype(BF16)

    arrive(main_r, 0)
    pack_v[...] = main_r[...].astype(F32).reshape(ROWS * 8, LANES)
    analyse = small_v[0, :64, :64]
    halves = []
    for p in range(2):
        rows = [pack_v[pl.ds(p * QUADS + q, ROWS, stride=8), :] for q in range(QUADS)]
        grid = jnp.concatenate(rows, axis=1).astype(BF16)
        part = mm(analyse, jnp.concatenate([grid, grid], axis=0))
        halves.extend(forward_twist(part[:32], part[32:]))
    lhs = jnp.concatenate(halves, axis=0)
    wide = mm(lhs, wave_high) + mm(lhs, wave_low)

    def spectrum(base):
        re_c, re_s = wide[base:base + 32, :COLS], wide[base:base + 32, COLS:]
        im_c, im_s = wide[base + 32:base + 64, :COLS], wide[base + 32:base + 64, COLS:]
        return re_c + im_s, im_c - re_s

    pre_re, pre_im = spectrum(0)
    dc_re, dc_im = spectrum(64)

    x_re = pre_re * dc_re + pre_im * dc_im
    x_im = pre_re * dc_im - pre_im * dc_re
    x_re, x_im = x_re.astype(BF16), x_im.astype(BF16)
    up_row = jnp.concatenate([x_re, -x_im], axis=1)
    mid_row = jnp.concatenate([x_im, x_re], axis=1)
    low_row = jnp.concatenate([-x_im, -x_re], axis=1)
    rhs = jnp.concatenate([up_row, mid_row, low_row, up_row], axis=0)
    back = mm_nt(wave_high, rhs) + mm_nt(wave_low, rhs)
    back = (back * turned_v[...]).astype(BF16)
    share = mm(jnp.concatenate([back, back], axis=1), small_v[3])
    share = share.reshape(ROWS, 2, 8, LANES)
    lane = lax.broadcasted_iota(jnp.int32, (ROWS, 8, LANES), 2)
    share = jnp.where(lane < 64, share[:, 0], share[:, 1])
    part_s[...] = pair(share)
    exchange(lambda s: part_s.at[lax.rem(plane + s, ROWS)], part_r, 2, plane_peer, ROWS, plane)
    keep(part_s.at[plane], part_r, 2, plane)

    arrive(taps_r, 1)
    taps = taps_r[...].astype(F32)
    taps = jnp.stack([jnp.where(lane < 64, taps, 0.0), jnp.where(lane < 64, 0.0, taps)], axis=1)
    taps = taps.reshape(COLS, LANES).astype(BF16)
    part = mm_nt(small_v[1, :64], taps) + mm_nt(small_v[1, 64:128], taps)
    lhs = jnp.concatenate(forward_twist(part[:32], part[32:]), axis=0)
    wide = mm(lhs, wave_high) + mm(lhs, wave_low)
    f_re, f_im = spectrum(0)

    products = [
        pre_re * f_re - pre_im * f_im,
        pre_re * f_im + pre_im * f_re,
        f_re * dc_re + f_im * dc_im,
        f_re * dc_im - f_im * dc_re,
    ]
    lhs = jnp.concatenate([product.astype(BF16) for product in products], axis=0)
    wide = mm(lhs, wave_high) + mm(lhs, wave_low)
    build = small_v[2, :32]
    for p in range(2):
        base = 64 * p
        re_c, re_s = wide[base:base + 32, :COLS], wide[base:base + 32, COLS:]
        im_c, im_s = wide[base + 32:base + 64, :COLS], wide[base + 32:base + 64, COLS:]
        half = jnp.concatenate(inverse_twist(re_c - im_s, re_s + im_c), axis=0)
        result = mm(build, jnp.concatenate([half, half], axis=0))
        for q in range(QUADS):
            pack_v[pl.ds(p * QUADS + q, ROWS, stride=8), :] = result[:, q * LANES:(q + 1) * LANES]
    back_s[...] = pack_v[...].reshape(ROWS, 8, LANES).astype(BF16)
    exchange(lambda s: back_s.at[lax.rem(me + s, ROWS)], back_r, 3, row_peer, ROWS, me)
    keep(back_s.at[me], back_r, 3, me)

    arrive(part_r, 2)
    total = jnp.sum(part_r[...].astype(F32), axis=0)
    lane = lax.broadcasted_iota(jnp.int32, (8, LANES), 1)
    total = total + jnp.where(lax.rem(lane, 64) < 32, pltpu.roll(total, 96, 1), pltpu.roll(total, 32, 1))
    sum_s[...] = pair(total)
    spot = dp * SLABS + z

    @pl.when(z == tensor)
    def _():
        keep(sum_s, sum_r, 4, spot)

    @pl.when(z != tensor)
    def _():
        send(sum_s, sum_r, 4, owner(0), spot)

    exchange(lambda s: sum_s, sum_r, 4, owner, COPIES, spot)

    arrive(back_r, 3)
    pack_v[...] = back_r[...].astype(F32).reshape(ROWS * 8, LANES)
    rows = [pack_v[pl.ds(n, ROWS, stride=8), :] for n in range(8)]
    conv = jnp.concatenate(rows[:QUADS], axis=1)
    out_ref[...] = (gate * conv).astype(BF16)
    gg_ref[...] = (up * conv).astype(BF16)
    gp_ref[...] = jnp.concatenate(rows[QUADS:], axis=1).astype(BF16)

    arrive(sum_r, 4)
    total = jnp.sum(sum_r[...].astype(F32), axis=0)
    total = total + pltpu.roll(total, 96, 1)
    gf_ref[0:8, :] = total[:, 0:32]
    gf_ref[8:16, :] = total[:, 64:96]

    left(main_r, 0, ROWS)
    left(taps_r, 1, ROWS)
    left(part_r, 2, ROWS)
    left(back_r, 3, ROWS)
    left(sum_r, 4, COPIES)

    @pl.when(z != tensor)
    def _():
        left(sum_r, 4, 2)


def hbm(*xs):
    return [pltpu.with_memory_space_constraint(x, pltpu.HBM) for x in xs]


def hand_over(a, b, c, d, a_out, b_out, c_out, d_out, sem):
    pairs = [(a, a_out), (b, b_out), (c, c_out), (d, d_out)]
    copies = [pltpu.make_async_copy(src, dst, sem.at[n]) for n, (src, dst) in enumerate(pairs)]
    for copy in copies:
        copy.start()
    for copy in copies:
        copy.wait()


def solution(mesh):
    norm = 1.0 / math.sqrt(mesh.size * POINTS)
    wave, twist, turned, small = make_tables(norm)

    def body(pregate, gate, upstream, filter_taps):
        block = jax.ShapeDtypeStruct((ROWS, COLS), BF16)
        message = pltpu.VMEM((ROWS, 8, LANES), BF16)
        results = pl.pallas_call(
            kernel,
            out_shape=[block, block, block, jax.ShapeDtypeStruct((16, ROWS), F32)],
            in_specs=[pl.BlockSpec(memory_space=pltpu.HBM)] * 8,
            out_specs=[pl.BlockSpec(memory_space=pltpu.VMEM)] * 4,
            scratch_shapes=[
                pltpu.VMEM((ROWS, COLS), BF16),
                pltpu.VMEM((ROWS, COLS), BF16),
                pltpu.VMEM((ROWS, COLS), BF16),
                pltpu.VMEM((16, ROWS), F32),
                pltpu.VMEM(wave.shape, BF16),
                pltpu.VMEM(twist.shape, F32),
                pltpu.VMEM(turned.shape, F32),
                pltpu.VMEM(small.shape, BF16),
                pltpu.VMEM((ROWS * 8, LANES), F32),
                message,
                message,
                pltpu.VMEM((8, LANES), BF16),
                message,
                message,
                message,
                message,
                message,
                pltpu.VMEM((8, LANES), BF16),
                pltpu.VMEM((COPIES, 8, LANES), BF16),
                pltpu.SemaphoreType.DMA((4,)),
                pltpu.SemaphoreType.DMA((4,)),
                pltpu.SemaphoreType.DMA((5,)),
                pltpu.SemaphoreType.DMA((5,)),
            ],
            compiler_params=pltpu.CompilerParams(
                collective_id=0, has_side_effects=True, vmem_limit_bytes=40 * 1024 * 1024
            ),
        )(
            *hbm(pregate.reshape(ROWS, COLS),
            gate.reshape(ROWS, COLS),
            upstream.reshape(ROWS, COLS),
            filter_taps.T,
            jnp.asarray(wave),
            jnp.asarray(twist),
            jnp.asarray(turned),
            jnp.asarray(small)),
        )
        results = pl.pallas_call(
            hand_over,
            out_shape=[block, block, block, jax.ShapeDtypeStruct((16, ROWS), F32)],
            in_specs=[pl.BlockSpec(memory_space=pl.ANY)] * 4,
            out_specs=[pl.BlockSpec(memory_space=pl.ANY)] * 4,
            scratch_shapes=[pltpu.SemaphoreType.DMA((4,))],
            compiler_params=pltpu.CompilerParams(vmem_limit_bytes=40 * 1024 * 1024),
        )(*results)
        shape = pregate.shape
        return tuple(value.reshape(shape) for value in results[:3]) + (results[3].T,)

    whole = P("dp", "tensor", "context")
    specs = (whole, whole, whole, P(None, "context"))
    return jax.shard_map(body, mesh=mesh, in_specs=specs, out_specs=specs, check_vma=False)
```

```python
import math

import jax
import jax.numpy as jnp
import ml_dtypes
import numpy as np
from jax import lax
from jax.experimental import pallas as pl
from jax.experimental.pallas import tpu as pltpu
from jax.sharding import PartitionSpec as P


COLS = 512
ROWS = 32
POINTS = ROWS * COLS
LANES = 128
QUADS = COLS // LANES
SLABS = 8
COPIES = 2 * SLABS
WORKERS = 16
F32 = jnp.float32
BF16 = jnp.bfloat16
MESH = pl.DeviceIdType.MESH


def split(table):
    high = table.astype(ml_dtypes.bfloat16)
    low = (table - high.astype(np.float64)).astype(ml_dtypes.bfloat16)
    return high, low


def make_tables(norm):
    r = np.arange(ROWS)
    k1 = np.arange(ROWS)
    c = np.arange(COLS)
    inner = 2.0 * np.pi * (np.outer(c, c) % COLS) / COLS
    wave = np.concatenate([np.cos(inner), np.sin(inner)], axis=1)
    wave = np.concatenate(split(wave), axis=0)
    wave = np.stack(np.split(wave, 2 * QUADS, axis=1))
    phase = 2.0 * np.pi * (np.outer(4 * k1 + 1, c) % (4 * POINTS)) / (4 * POINTS)
    twist = np.stack([np.cos(phase), np.sin(phase)]).astype(np.float32)
    turned = np.concatenate([np.cos(phase.T)] * 2 + [np.sin(phase.T)] * 2, axis=1).astype(np.float32)
    outer = 2.0 * np.pi * (np.outer(4 * k1 + 1, r) % (4 * ROWS)) / (4 * ROWS)
    first = np.concatenate([np.cos(outer), -np.sin(outer)], axis=0)
    first_high, first_low = split(first)
    analyse = np.concatenate([first_high, first_low], axis=1)
    analyse_taps = np.concatenate(
        [np.concatenate([first_high] * 4, axis=1), np.concatenate([first_low] * 4, axis=1)], axis=0
    )
    last_high, last_low = split(first.T / POINTS)
    build = np.concatenate([last_high, last_low], axis=1)
    wide = np.concatenate([first * (norm / POINTS)] * 2, axis=0)
    wide = np.concatenate([wide] * 4, axis=1)
    build_taps = np.concatenate(split(wide), axis=0)
    small = np.zeros((5, 256, LANES), ml_dtypes.bfloat16)
    small[0, :64, :64] = analyse
    small[1, :128] = analyse_taps
    small[2, :32] = build
    small[3, :256] = build_taps
    return wave, twist, turned, small[:4]


def mm(a, b):
    return jnp.dot(a, b, preferred_element_type=F32)


def mm_nt(a, b):
    return lax.dot_general(a, b, (((1,), (1,)), ((), ())), preferred_element_type=F32)


def pair(value):
    lane = lax.broadcasted_iota(jnp.int32, value.shape, value.ndim - 1)
    high = value.astype(BF16).astype(F32)
    return jnp.where(lax.rem(lane, 64) < 32, high, value - high).astype(BF16)


def kernel(
    pre_hbm, gate_hbm, up_hbm, taps_hbm, wave_hbm, twist_hbm, turned_hbm, small_hbm,
    out_ref, gg_ref, gp_ref, gf_ref,
    pre_v, gate_v, up_v, taps_v, wave_v, twist_v, turned_v, small_v, pack_v,
    main_s, main_r, taps_s, taps_r, back_s, back_r, part_s, part_r, sum_s, sum_r,
    in_sem, table_sem, send_sem, recv_sem,
):
    dp = lax.axis_index("dp")
    tensor = lax.axis_index("tensor")
    me = lax.axis_index("context")
    x, z = me // SLABS, lax.rem(me, SLABS)
    plane = x * SLABS + tensor
    side = z // 4
    worker = (z >= 2) & (z < 6)
    idle = (z < 2) | (z >= 6)
    mine = x * 4 + z - 2

    def row_peer(step):
        mirrored = z + side * (7 - 2 * z)
        far = 7 - step // 4
        far = far - (mirrored - far + 8) // 8
        far = far + step // 28 * (mirrored - far)
        return (dp, tensor, lax.rem(x + 3 - lax.rem(step, 4), 4) * SLABS + far + side * (7 - 2 * far))

    def worker_place(step):
        far = 5 - step // 4
        return lax.rem(x + 3 - lax.rem(step, 4), 4), far + side * (7 - 2 * far)

    def worker_peer(step):
        wx, wz = worker_place(step)
        return (dp, tensor, wx * SLABS + wz)

    def tensor_peer(step):
        return (dp, lax.rem(tensor + step, SLABS), me)

    def plane_place(step):
        return lax.rem(plane + 1 + lax.rem(step + 19, ROWS - 1), ROWS)

    def plane_peer(step):
        other = plane_place(step)
        return (dp, lax.rem(other, SLABS), other // SLABS * SLABS + z)

    def owner(step):
        return (1 - dp, lax.rem(tensor + 4 + step, SLABS), plane)

    def near_owner(step):
        return (dp, lax.rem(tensor + step, SLABS), plane)

    barrier = pltpu.get_barrier_semaphore()

    def greet(peers, start, stop):
        def signal(step, carry):
            pl.semaphore_signal(barrier, inc=1, device_id=peers(step), device_id_type=MESH)
            return carry

        lax.fori_loop(start, stop, signal, 0)

    @pl.when(worker)
    def _():
        greet(row_peer, 0, ROWS - 1)

    @pl.when(idle)
    def _():
        greet(worker_peer, 0, WORKERS)

    greet(lambda step: (1 - dp, tensor, me), 0, 1)
    greet(tensor_peer, 1, SLABS)

    loads = [
        pltpu.make_async_copy(src, dst, in_sem.at[n])
        for n, (src, dst) in enumerate(
            [(pre_hbm, pre_v), (gate_hbm, gate_v), (up_hbm, up_v), (taps_hbm, taps_v)]
        )
    ]
    tables = [
        pltpu.make_async_copy(src, dst, table_sem.at[n])
        for n, (src, dst) in enumerate(
            [(small_hbm, small_v), (twist_hbm, twist_v), (wave_hbm, wave_v), (turned_hbm, turned_v)]
        )
    ]
    for copy in loads:
        copy.start()
    for copy in tables:
        copy.start()
    for copy in loads:
        copy.wait()

    gate = gate_v[...].astype(F32)
    up = up_v[...].astype(F32)
    dconv = (up * gate).astype(BF16).astype(F32)
    pre = pre_v[...].astype(F32)
    for p, signal in enumerate((pre, dconv)):
        for q in range(QUADS):
            pack_v[pl.ds(p * QUADS + q, ROWS, stride=8), :] = signal[:, q * LANES:(q + 1) * LANES]
    main_s[...] = pack_v[:ROWS * 8].reshape(WORKERS, 16, LANES).astype(BF16)

    taps = taps_v[...]
    taps_high = taps.astype(BF16).astype(F32)
    taps_low = taps - taps_high
    taps_s[...] = jnp.concatenate(
        [taps_high[:8], taps_low[:8], taps_high[8:], taps_low[8:]], axis=1
    ).astype(BF16)

    @pl.when(worker)
    def _():
        pl.semaphore_wait(barrier, ROWS - 1 + SLABS)

    @pl.when(idle)
    def _():
        pl.semaphore_wait(barrier, WORKERS + SLABS)

    def send(source, target, phase, peer, slot):
        pltpu.make_async_remote_copy(
            src_ref=source,
            dst_ref=target.at[slot],
            send_sem=send_sem.at[phase],
            recv_sem=recv_sem.at[phase],
            device_id=peer,
            device_id_type=MESH,
        ).start()

    def exchange(source, target, phase, peers, start, stop, slot):
        def one(step, carry):
            send(source(step), target, phase, peers(step), slot)
            return carry

        lax.fori_loop(start, stop, one, 0)

    def keep(source, target, phase, slot):
        pltpu.make_async_copy(source, target.at[slot], recv_sem.at[phase]).start()

    def arrive(target, phase):
        pltpu.make_async_copy(target, target, recv_sem.at[phase]).wait()

    def left(target, phase, count):
        part = target.at[pl.ds(0, count)]
        pltpu.make_async_copy(part, part, send_sem.at[phase]).wait()

    def to_workers(source, target, phase):
        def one(step, carry):
            wx, wz = worker_place(step)

            @pl.when((wx != x) | (wz != z))
            def _():
                send(source(wx * 4 + wz - 2), target, phase, worker_peer(step), me)

            return carry

        lax.fori_loop(0, WORKERS, one, 0)

    to_workers(lambda w: main_s.at[w], main_r, 0)
    to_workers(lambda w: taps_s, taps_r, 1)

    for copy in tables:
        copy.wait()

    @pl.when(worker)
    def _():
        keep(main_s.at[mine], main_r, 0, me)
        keep(taps_s, taps_r, 1, me)
        wave_high = jnp.concatenate([wave_v[n, :COLS] for n in range(2 * QUADS)], axis=1)
        wave_low = jnp.concatenate([wave_v[n, COLS:] for n in range(2 * QUADS)], axis=1)
        cos = twist_v[0]
        sin = twist_v[1]

        def forward_twist(re, im):
            return (re * cos + im * sin).astype(BF16), (im * cos - re * sin).astype(BF16)

        def inverse_twist(re, im):
            return (re * cos - im * sin).astype(BF16), (re * sin + im * cos).astype(BF16)

        arrive(main_r, 0)
        pack_v[...] = main_r[...].astype(F32).reshape(ROWS * 16, LANES)
        analyse = small_v[0, :64, :64]
        halves = []
        for n in range(4):
            rows = [pack_v[pl.ds(n * QUADS + q, ROWS, stride=16), :] for q in range(QUADS)]
            grid = jnp.concatenate(rows, axis=1).astype(BF16)
            part = mm(analyse, jnp.concatenate([grid, grid], axis=0))
            halves.extend(forward_twist(part[:32], part[32:]))
        lhs = jnp.concatenate(halves, axis=0)
        wide = mm(lhs, wave_high) + mm(lhs, wave_low)

        def spectrum(base):
            re_c, re_s = wide[base:base + 32, :COLS], wide[base:base + 32, COLS:]
            im_c, im_s = wide[base + 32:base + 64, :COLS], wide[base + 32:base + 64, COLS:]
            return re_c + im_s, im_c - re_s

        specs = [spectrum(64 * n) for n in range(4)]

        x_re = x_im = 0.0
        for (pre_re, pre_im), (dc_re, dc_im) in (specs[:2], specs[2:]):
            x_re = x_re + pre_re * dc_re + pre_im * dc_im
            x_im = x_im + pre_re * dc_im - pre_im * dc_re
        x_re, x_im = x_re.astype(BF16), x_im.astype(BF16)
        up_row = jnp.concatenate([x_re, -x_im], axis=1)
        mid_row = jnp.concatenate([x_im, x_re], axis=1)
        low_row = jnp.concatenate([-x_im, -x_re], axis=1)
        rhs = jnp.concatenate([up_row, mid_row, low_row, up_row], axis=0)
        back = mm_nt(wave_high, rhs)
        back = (back * turned_v[...]).astype(BF16)
        share = mm(jnp.concatenate([back, back], axis=1), small_v[3])
        share = share.reshape(ROWS, 2, 8, LANES)
        lane = lax.broadcasted_iota(jnp.int32, (ROWS, 8, LANES), 2)
        share = jnp.where(lane < 64, share[:, 0], share[:, 1])
        part_s[...] = pair(share)
        exchange(lambda s: part_s.at[plane_place(s)], part_r, 2, plane_peer, 0, ROWS - 1, plane)
        keep(part_s.at[plane], part_r, 2, plane)

        arrive(taps_r, 1)
        taps = taps_r[...].astype(F32)
        taps = jnp.stack([jnp.where(lane < 64, taps, 0.0), jnp.where(lane < 64, 0.0, taps)], axis=1)
        taps = taps.reshape(COLS, LANES).astype(BF16)
        part = mm_nt(small_v[1, :64], taps) + mm_nt(small_v[1, 64:128], taps)
        lhs = jnp.concatenate(forward_twist(part[:32], part[32:]), axis=0)
        wide = mm(lhs, wave_high) + mm(lhs, wave_low)
        f_re, f_im = spectrum(0)

        products = []
        for (pre_re, pre_im), (dc_re, dc_im) in (specs[:2], specs[2:]):
            products += [
                pre_re * f_re - pre_im * f_im,
                pre_re * f_im + pre_im * f_re,
                f_re * dc_re + f_im * dc_im,
                f_re * dc_im - f_im * dc_re,
            ]
        lhs = jnp.concatenate([product.astype(BF16) for product in products], axis=0)
        wide = mm(lhs, wave_high) + mm(lhs, wave_low)
        build = small_v[2, :32]
        for n in range(4):
            base = 64 * n
            re_c, re_s = wide[base:base + 32, :COLS], wide[base:base + 32, COLS:]
            im_c, im_s = wide[base + 32:base + 64, :COLS], wide[base + 32:base + 64, COLS:]
            half = jnp.concatenate(inverse_twist(re_c - im_s, re_s + im_c), axis=0)
            result = mm(build, jnp.concatenate([half, half], axis=0))
            for q in range(QUADS):
                pack_v[pl.ds(n * QUADS + q, ROWS, stride=16), :] = result[:, q * LANES:(q + 1) * LANES]
        back_s[...] = pack_v[...].reshape(ROWS, 16, LANES).astype(BF16)
        exchange(lambda s: back_s.at[row_peer(s)[2]], back_r, 3, row_peer, 0, ROWS - 1, mine)
        keep(back_s.at[me], back_r, 3, mine)

        arrive(part_r, 2)
        total = jnp.sum(part_r[...].astype(F32), axis=0)
        lane = lax.broadcasted_iota(jnp.int32, (8, LANES), 1)
        total = total + jnp.where(lax.rem(lane, 64) < 32, pltpu.roll(total, 96, 1), pltpu.roll(total, 32, 1))
        sum_s[...] = pair(total)
        spot = dp * 4 + z - 2
        exchange(lambda s: sum_s, sum_r, 4, owner, 0, SLABS, spot)
        exchange(lambda s: sum_s, sum_r, 4, near_owner, 1, SLABS, spot)

        @pl.when(z == tensor)
        def _():
            keep(sum_s, sum_r, 4, spot)

        @pl.when(z != tensor)
        def _():
            send(sum_s, sum_r, 4, near_owner(0), spot)

    arrive(back_r, 3)
    pack_v[:ROWS * 8] = back_r[...].astype(F32).reshape(ROWS * 8, LANES)
    rows = [pack_v[pl.ds(n, ROWS, stride=8), :] for n in range(8)]
    conv = jnp.concatenate(rows[:QUADS], axis=1)
    out_ref[...] = (gate * conv).astype(BF16)
    gg_ref[...] = (up * conv).astype(BF16)
    gp_ref[...] = jnp.concatenate(rows[QUADS:], axis=1).astype(BF16)

    arrive(sum_r, 4)
    total = jnp.sum(sum_r[...].astype(F32), axis=0)
    total = total + pltpu.roll(total, 96, 1)
    gf_ref[0:8, :] = total[:, 0:32]
    gf_ref[8:16, :] = total[:, 64:96]

    left(main_r, 0, WORKERS - 1)
    left(taps_r, 1, WORKERS - 1)

    @pl.when(idle)
    def _():
        left(main_r, 0, 1)
        left(taps_r, 1, 1)

    @pl.when(worker)
    def _():
        left(part_r, 2, ROWS - 1)
        left(back_s, 3, ROWS - 1)
        left(part_r, 4, COPIES - 1)

        @pl.when(z != tensor)
        def _():
            left(part_r, 4, 1)


def hbm(*xs):
    return [pltpu.with_memory_space_constraint(x, pltpu.HBM) for x in xs]


def hand_over(a, b, c, d, a_out, b_out, c_out, d_out, sem):
    pairs = [(a, a_out), (b, b_out), (c, c_out), (d, d_out)]
    copies = [pltpu.make_async_copy(src, dst, sem.at[n]) for n, (src, dst) in enumerate(pairs)]
    for copy in copies:
        copy.start()
    for copy in copies:
        copy.wait()


def solution(mesh):
    norm = 1.0 / math.sqrt(mesh.size * POINTS)
    wave, twist, turned, small = make_tables(norm)

    def body(pregate, gate, upstream, filter_taps):
        block = jax.ShapeDtypeStruct((ROWS, COLS), BF16)
        message = pltpu.VMEM((ROWS, 8, LANES), BF16)
        results = pl.pallas_call(
            kernel,
            out_shape=[block, block, block, jax.ShapeDtypeStruct((16, ROWS), F32)],
            in_specs=[pl.BlockSpec(memory_space=pltpu.HBM)] * 8,
            out_specs=[pl.BlockSpec(memory_space=pltpu.VMEM)] * 4,
            scratch_shapes=[
                pltpu.VMEM((ROWS, COLS), BF16),
                pltpu.VMEM((ROWS, COLS), BF16),
                pltpu.VMEM((ROWS, COLS), BF16),
                pltpu.VMEM((16, ROWS), F32),
                pltpu.VMEM(wave.shape, BF16),
                pltpu.VMEM(twist.shape, F32),
                pltpu.VMEM(turned.shape, F32),
                pltpu.VMEM(small.shape, BF16),
                pltpu.VMEM((ROWS * 16, LANES), F32),
                pltpu.VMEM((WORKERS, 16, LANES), BF16),
                pltpu.VMEM((ROWS, 16, LANES), BF16),
                pltpu.VMEM((8, LANES), BF16),
                message,
                pltpu.VMEM((ROWS, 16, LANES), BF16),
                pltpu.VMEM((WORKERS, 16, LANES), BF16),
                message,
                message,
                pltpu.VMEM((8, LANES), BF16),
                pltpu.VMEM((8, 8, LANES), BF16),
                pltpu.SemaphoreType.DMA((4,)),
                pltpu.SemaphoreType.DMA((4,)),
                pltpu.SemaphoreType.DMA((5,)),
                pltpu.SemaphoreType.DMA((5,)),
            ],
            compiler_params=pltpu.CompilerParams(
                collective_id=0, has_side_effects=True, vmem_limit_bytes=40 * 1024 * 1024
            ),
        )(
            *hbm(pregate.reshape(ROWS, COLS),
            gate.reshape(ROWS, COLS),
            upstream.reshape(ROWS, COLS),
            filter_taps.T,
            jnp.asarray(wave),
            jnp.asarray(twist),
            jnp.asarray(turned),
            jnp.asarray(small)),
        )
        results = pl.pallas_call(
            hand_over,
            out_shape=[block, block, block, jax.ShapeDtypeStruct((16, ROWS), F32)],
            in_specs=[pl.BlockSpec(memory_space=pl.ANY)] * 4,
            out_specs=[pl.BlockSpec(memory_space=pl.ANY)] * 4,
            scratch_shapes=[pltpu.SemaphoreType.DMA((4,))],
            compiler_params=pltpu.CompilerParams(vmem_limit_bytes=40 * 1024 * 1024),
        )(*results)
        shape = pregate.shape
        return tuple(value.reshape(shape) for value in results[:3]) + (results[3].T,)

    whole = P("dp", "tensor", "context")
    specs = (whole, whole, whole, P(None, "context"))
    return jax.shard_map(body, mesh=mesh, in_specs=specs, out_specs=specs, check_vma=False)
```

```python
import math

import jax
import jax.numpy as jnp
import ml_dtypes
import numpy as np
from jax import lax
from jax.experimental import pallas as pl
from jax.experimental.pallas import tpu as pltpu
from jax.sharding import PartitionSpec as P


COLS = 512
ROWS = 32
POINTS = ROWS * COLS
LANES = 128
QUADS = COLS // LANES
SLABS = 8
COPIES = 2 * SLABS
WORKERS = 16
F32 = jnp.float32
BF16 = jnp.bfloat16
MESH = pl.DeviceIdType.MESH


def split(table):
    high = table.astype(ml_dtypes.bfloat16)
    low = (table - high.astype(np.float64)).astype(ml_dtypes.bfloat16)
    return high, low


def make_tables(norm):
    r = np.arange(ROWS)
    k1 = np.arange(ROWS)
    c = np.arange(COLS)
    inner = 2.0 * np.pi * (np.outer(c, c) % COLS) / COLS
    wave = np.concatenate([np.cos(inner), np.sin(inner)], axis=1)
    wave = np.concatenate(split(wave), axis=0)
    wave = np.stack(np.split(wave, 2 * QUADS, axis=1))
    phase = 2.0 * np.pi * (np.outer(4 * k1 + 1, c) % (4 * POINTS)) / (4 * POINTS)
    twist = np.stack([np.cos(phase), np.sin(phase)]).astype(np.float32)
    turned = np.concatenate([np.cos(phase.T)] * 2 + [np.sin(phase.T)] * 2, axis=1).astype(np.float32)
    outer = 2.0 * np.pi * (np.outer(4 * k1 + 1, r) % (4 * ROWS)) / (4 * ROWS)
    first = np.concatenate([np.cos(outer), -np.sin(outer)], axis=0)
    first_high, first_low = split(first)
    analyse = np.concatenate([first_high, first_low], axis=1)
    analyse_taps = np.concatenate(
        [np.concatenate([first_high] * 4, axis=1), np.concatenate([first_low] * 4, axis=1)], axis=0
    )
    last_high, last_low = split(first.T / POINTS)
    build = np.concatenate([last_high, last_low], axis=1)
    wide = np.concatenate([first * (norm / POINTS)] * 2, axis=0)
    wide = np.concatenate([wide] * 4, axis=1)
    build_taps = np.concatenate(split(wide), axis=0)
    small = np.zeros((5, 256, LANES), ml_dtypes.bfloat16)
    small[0, :64, :64] = analyse
    small[1, :128] = analyse_taps
    small[2, :32] = build
    small[3, :256] = build_taps
    return wave, twist, turned, small[:4]


def mm(a, b):
    return jnp.dot(a, b, preferred_element_type=F32)


def mm_nt(a, b):
    return lax.dot_general(a, b, (((1,), (1,)), ((), ())), preferred_element_type=F32)


def pair(value):
    lane = lax.broadcasted_iota(jnp.int32, value.shape, value.ndim - 1)
    high = value.astype(BF16).astype(F32)
    return jnp.where(lax.rem(lane, 64) < 32, high, value - high).astype(BF16)


def kernel(
    pre_hbm, gate_hbm, up_hbm, taps_hbm, wave_hbm, twist_hbm, turned_hbm, small_hbm,
    out_ref, gg_ref, gp_ref, gf_ref,
    pre_v, gate_v, up_v, taps_v, wave_v, twist_v, turned_v, small_v, pack_v, spec_v,
    main_s, main_r, taps_s, taps_r, back_s, back_r, part_s, part_r, sum_s, sum_r,
    in_sem, table_sem, send_sem, recv_sem, ready_sem,
):
    dp = lax.axis_index("dp")
    tensor = lax.axis_index("tensor")
    me = lax.axis_index("context")
    x, z = me // SLABS, lax.rem(me, SLABS)
    plane = x * SLABS + tensor
    side = z // 4
    worker = (z >= 2) & (z < 6)
    idle = (z < 2) | (z >= 6)
    mine = x * 4 + z - 2

    def row_peer(step):
        mirrored = z + side * (7 - 2 * z)
        far = 7 - step // 4
        far = far - (mirrored - far + 8) // 8
        far = far + step // 28 * (mirrored - far)
        return (dp, tensor, lax.rem(x + 3 - lax.rem(step, 4), 4) * SLABS + far + side * (7 - 2 * far))

    def worker_place(step):
        far = 5 - step // 4
        return lax.rem(x + 3 - lax.rem(step, 4), 4), far + side * (7 - 2 * far)

    def worker_peer(step):
        wx, wz = worker_place(step)
        return (dp, tensor, wx * SLABS + wz)

    def tensor_peer(step):
        return (dp, lax.rem(tensor + step, SLABS), me)

    def plane_place(step):
        return lax.rem(x + 3 - lax.rem(step, 4), 4), step // 4

    def owner(step):
        return (1 - dp, lax.rem(tensor + 1 + step, SLABS), plane)

    def near_owner(step):
        return (dp, lax.rem(tensor + step, SLABS), plane)

    def sum_peer(step):
        return (1 - dp, z, x * SLABS + 2 + step)

    barrier = pltpu.get_barrier_semaphore()

    def greet(peers, start, stop):
        def signal(step, carry):
            pl.semaphore_signal(barrier, inc=1, device_id=peers(step), device_id_type=MESH)
            return carry

        lax.fori_loop(start, stop, signal, 0)

    @pl.when(dp == 0)
    def _():
        greet(sum_peer, 0, 4)

        @pl.when(worker)
        def _():
            greet(owner, 0, SLABS)

    @pl.when(worker)
    def _():
        greet(row_peer, 0, ROWS - 1)

    @pl.when(idle)
    def _():
        greet(worker_peer, 0, WORKERS)

    greet(tensor_peer, 1, SLABS)

    loads = [
        pltpu.make_async_copy(src, dst, in_sem.at[n])
        for n, (src, dst) in enumerate(
            [(pre_hbm, pre_v), (gate_hbm, gate_v), (up_hbm, up_v), (taps_hbm, taps_v)]
        )
    ]
    tables = [
        pltpu.make_async_copy(src, dst, table_sem.at[n])
        for n, (src, dst) in enumerate(
            [(small_hbm, small_v), (twist_hbm, twist_v), (wave_hbm, wave_v), (turned_hbm, turned_v)]
        )
    ]
    for copy in loads:
        copy.start()
    for copy in tables:
        copy.start()
    for copy in loads:
        copy.wait()

    gate = gate_v[...].astype(F32)
    up = up_v[...].astype(F32)
    dconv = (up * gate).astype(BF16).astype(F32)
    pre = pre_v[...].astype(F32)
    for p, signal in enumerate((pre, dconv)):
        for q in range(QUADS):
            pack_v[pl.ds(p * QUADS + q, ROWS, stride=8), :] = signal[:, q * LANES:(q + 1) * LANES]
    main_s[...] = pack_v[:ROWS * 8].reshape(WORKERS, 16, LANES).astype(BF16)

    taps = taps_v[...]
    taps_high = taps.astype(BF16).astype(F32)
    taps_low = taps - taps_high
    taps_s[...] = jnp.concatenate(
        [taps_high[:8], taps_low[:8], taps_high[8:], taps_low[8:]], axis=1
    ).astype(BF16)

    for condition, count in (
        (worker & (dp == 0), ROWS - 1 + SLABS - 1),
        (idle & (dp == 0), WORKERS + SLABS - 1),
        (worker & (dp == 1), ROWS - 1 + SLABS - 1 + SLABS + 4),
        (idle & (dp == 1), WORKERS + SLABS - 1 + 4),
    ):
        @pl.when(condition)
        def _(count=count):
            pl.semaphore_wait(barrier, count)

    def send(source, target, phase, peer, slot):
        pltpu.make_async_remote_copy(
            src_ref=source,
            dst_ref=target.at[slot],
            send_sem=send_sem.at[phase],
            recv_sem=recv_sem.at[phase],
            device_id=peer,
            device_id_type=MESH,
        ).start()

    def exchange(source, target, phase, peers, start, stop, slot):
        def one(step, carry):
            send(source(step), target, phase, peers(step), slot)
            return carry

        lax.fori_loop(start, stop, one, 0)

    def keep(source, target, phase, slot):
        pltpu.make_async_copy(source, target.at[slot], recv_sem.at[phase]).start()

    def arrive(target, phase):
        pltpu.make_async_copy(target, target, recv_sem.at[phase]).wait()

    def left(target, phase, count):
        part = target.at[pl.ds(0, count)]
        pltpu.make_async_copy(part, part, send_sem.at[phase]).wait()

    def to_workers(source, target, phase):
        def one(step, carry):
            wx, wz = worker_place(step)

            @pl.when((wx != x) | (wz != z))
            def _():
                send(source(wx * 4 + wz - 2), target, phase, worker_peer(step), me)

            return carry

        lax.fori_loop(0, WORKERS, one, 0)

    block = z * 4 + x
    first = lax.rem(tensor - z + SLABS, SLABS)
    own_taps = worker & (lax.rem(mine + SLABS, SLABS) == first)
    for w in (first, first + SLABS):
        @pl.when((w != mine) | idle)
        def _(w=w):
            send(taps_s, taps_r, 1, (dp, tensor, w // 4 * SLABS + 2 + lax.rem(w, 4)), block)

    to_workers(lambda w: main_s.at[w], main_r, 0)

    @pl.when(dp == 1)
    def _():
        def signal(step, carry):
            pl.semaphore_signal(ready_sem, inc=1, device_id=sum_peer(step), device_id_type=MESH)
            return carry

        lax.fori_loop(0, 4, signal, 0)

    for copy in tables:
        copy.wait()

    @pl.when(worker)
    def _():
        keep(main_s.at[mine], main_r, 0, me)
        slab = lax.rem(tensor + COPIES - mine, SLABS)
        held = taps_r.at[pl.ds(slab * 4, 4)]

        @pl.when(own_taps)
        def _():
            keep(taps_s, taps_r, 1, block)

        arrive(held, 1)
        exchange(lambda s: held, taps_r, 5, tensor_peer, 1, SLABS, pl.ds(slab * 4, 4))
        wave_high = jnp.concatenate([wave_v[n, :COLS] for n in range(2 * QUADS)], axis=1)
        wave_low = jnp.concatenate([wave_v[n, COLS:] for n in range(2 * QUADS)], axis=1)
        cos = twist_v[0]
        sin = twist_v[1]

        def forward_twist(re, im):
            return (re * cos + im * sin).astype(BF16), (im * cos - re * sin).astype(BF16)

        def inverse_twist(re, im):
            return (re * cos - im * sin).astype(BF16), (re * sin + im * cos).astype(BF16)

        arrive(main_r, 0)
        pack_v[...] = main_r[...].astype(F32).reshape(ROWS * 16, LANES)
        analyse = small_v[0, :64, :64]
        halves = []
        for n in range(4):
            rows = [pack_v[pl.ds(n * QUADS + q, ROWS, stride=16), :] for q in range(QUADS)]
            grid = jnp.concatenate(rows, axis=1).astype(BF16)
            part = mm(analyse, jnp.concatenate([grid, grid], axis=0))
            halves.extend(forward_twist(part[:32], part[32:]))
        lhs = jnp.concatenate(halves, axis=0)
        wide = mm(lhs, wave_high) + mm(lhs, wave_low)

        def spectrum(wide, base):
            re_c, re_s = wide[base:base + 32, :COLS], wide[base:base + 32, COLS:]
            im_c, im_s = wide[base + 32:base + 64, :COLS], wide[base + 32:base + 64, COLS:]
            return re_c + im_s, im_c - re_s

        for n in range(4):
            spec_v[2 * n], spec_v[2 * n + 1] = spectrum(wide, 64 * n)

        def shares():
            specs = [(spec_v[2 * n], spec_v[2 * n + 1]) for n in range(4)]
            x_re = x_im = 0.0
            for (pre_re, pre_im), (dc_re, dc_im) in (specs[:2], specs[2:]):
                x_re = x_re + pre_re * dc_re + pre_im * dc_im
                x_im = x_im + pre_re * dc_im - pre_im * dc_re
            x_re, x_im = x_re.astype(BF16), x_im.astype(BF16)
            up_row = jnp.concatenate([x_re, -x_im], axis=1)
            mid_row = jnp.concatenate([x_im, x_re], axis=1)
            low_row = jnp.concatenate([-x_im, -x_re], axis=1)
            rhs = jnp.concatenate([up_row, mid_row, low_row, up_row], axis=0)
            back = mm_nt(wave_high, rhs)
            back = (back * turned_v[...]).astype(BF16)
            share = mm(jnp.concatenate([back, back], axis=1), small_v[3])
            share = share.reshape(ROWS, 2, 8, LANES)
            lane = lax.broadcasted_iota(jnp.int32, (ROWS, 8, LANES), 2)
            share = jnp.where(lane < 64, share[:, 0], share[:, 1])
            part_s[...] = pair(share)

            def one(step, carry):
                px, pt = plane_place(step)

                @pl.when((px != x) | (pt != tensor))
                def _():
                    send(part_s.at[px * SLABS + pt], part_r, 2, (dp, pt, px * SLABS + z), plane)

                return carry

            lax.fori_loop(0, ROWS, one, 0)
            keep(part_s.at[plane], part_r, 2, plane)

        def convolutions():
            specs = [(spec_v[2 * n], spec_v[2 * n + 1]) for n in range(4)]
            lane = lax.broadcasted_iota(jnp.int32, (ROWS, 8, LANES), 2)
            arrive(taps_r.at[pl.ds(0, ROWS - 4)], 5)
            taps = taps_r[...].astype(F32).reshape(SLABS, 4, 8, LANES)
            taps = jnp.stack([taps[n % SLABS, n // SLABS] for n in range(ROWS)])
            taps = jnp.stack([jnp.where(lane < 64, taps, 0.0), jnp.where(lane < 64, 0.0, taps)], axis=1)
            taps = taps.reshape(COLS, LANES).astype(BF16)
            part = mm_nt(small_v[1, :64], taps) + mm_nt(small_v[1, 64:128], taps)
            lhs = jnp.concatenate(forward_twist(part[:32], part[32:]), axis=0)
            wide = mm(lhs, wave_high) + mm(lhs, wave_low)
            f_re, f_im = spectrum(wide, 0)

            products = []
            for (pre_re, pre_im), (dc_re, dc_im) in (specs[:2], specs[2:]):
                products += [
                    pre_re * f_re - pre_im * f_im,
                    pre_re * f_im + pre_im * f_re,
                    f_re * dc_re + f_im * dc_im,
                    f_re * dc_im - f_im * dc_re,
                ]
            lhs = jnp.concatenate([product.astype(BF16) for product in products], axis=0)
            wide = mm(lhs, wave_high) + mm(lhs, wave_low)
            build = small_v[2, :32]
            for n in range(4):
                base = 64 * n
                re_c, re_s = wide[base:base + 32, :COLS], wide[base:base + 32, COLS:]
                im_c, im_s = wide[base + 32:base + 64, :COLS], wide[base + 32:base + 64, COLS:]
                half = jnp.concatenate(inverse_twist(re_c - im_s, re_s + im_c), axis=0)
                result = mm(build, jnp.concatenate([half, half], axis=0))
                for q in range(QUADS):
                    pack_v[pl.ds(n * QUADS + q, ROWS, stride=16), :] = result[:, q * LANES:(q + 1) * LANES]
            back_s[...] = pack_v[...].reshape(ROWS, 16, LANES).astype(BF16)
            keep(back_s.at[me], back_r, 3, mine)
            exchange(lambda s: back_s.at[row_peer(s)[2]], back_r, 3, row_peer, 0, ROWS - 1, mine)

        def sums():
            arrive(part_r, 2)
            total = jnp.sum(part_r[...].astype(F32), axis=0)
            lane = lax.broadcasted_iota(jnp.int32, (8, LANES), 1)
            total = total + jnp.where(lax.rem(lane, 64) < 32, pltpu.roll(total, 96, 1), pltpu.roll(total, 32, 1))
            sum_s[...] = pair(total)
            spot = dp * 4 + z - 2

            @pl.when(dp == 1)
            def _():
                exchange(lambda s: sum_s, sum_r, 4, owner, 0, SLABS, spot)

            exchange(lambda s: sum_s, sum_r, 4, near_owner, 1, SLABS, spot)

            @pl.when(z == tensor)
            def _():
                keep(sum_s, sum_r, 4, spot)

            @pl.when(z != tensor)
            def _():
                send(sum_s, sum_r, 4, near_owner(0), spot)

            @pl.when(dp == 0)
            def _():
                pl.semaphore_wait(ready_sem, SLABS)
                exchange(lambda s: sum_s, sum_r, 4, owner, 0, SLABS, spot)

        @pl.when(dp == 0)
        def _():
            convolutions()
            shares()
            sums()

        @pl.when(dp == 1)
        def _():
            shares()
            sums()
            convolutions()

    arrive(back_r, 3)
    pack_v[:ROWS * 8] = back_r[...].astype(F32).reshape(ROWS * 8, LANES)
    rows = [pack_v[pl.ds(n, ROWS, stride=8), :] for n in range(8)]
    conv = jnp.concatenate(rows[:QUADS], axis=1)
    out_ref[...] = (gate * conv).astype(BF16)
    gg_ref[...] = (up * conv).astype(BF16)
    gp_ref[...] = jnp.concatenate(rows[QUADS:], axis=1).astype(BF16)

    arrive(sum_r, 4)
    total = jnp.sum(sum_r[...].astype(F32), axis=0)
    total = total + pltpu.roll(total, 96, 1)
    gf_ref[0:8, :] = total[:, 0:32]
    gf_ref[8:16, :] = total[:, 64:96]

    left(main_r, 0, WORKERS - 1)
    left(taps_r, 1, 1)

    @pl.when(idle)
    def _():
        left(main_r, 0, 1)

    @pl.when(jnp.logical_not(own_taps))
    def _():
        left(taps_r, 1, 1)

    @pl.when(worker)
    def _():
        left(taps_r, 5, ROWS - 4)
        left(part_r, 2, ROWS - 1)
        left(back_s, 3, ROWS - 1)
        left(part_r, 4, COPIES - 1)

        @pl.when(z != tensor)
        def _():
            left(part_r, 4, 1)


def hbm(*xs):
    return [pltpu.with_memory_space_constraint(x, pltpu.HBM) for x in xs]


def hand_over(a, b, c, d, a_out, b_out, c_out, d_out, sem):
    pairs = [(a, a_out), (b, b_out), (c, c_out), (d, d_out)]
    copies = [pltpu.make_async_copy(src, dst, sem.at[n]) for n, (src, dst) in enumerate(pairs)]
    for copy in copies:
        copy.start()
    for copy in copies:
        copy.wait()


def solution(mesh):
    norm = 1.0 / math.sqrt(mesh.size * POINTS)
    wave, twist, turned, small = make_tables(norm)

    def body(pregate, gate, upstream, filter_taps):
        block = jax.ShapeDtypeStruct((ROWS, COLS), BF16)
        message = pltpu.VMEM((ROWS, 8, LANES), BF16)
        results = pl.pallas_call(
            kernel,
            out_shape=[block, block, block, jax.ShapeDtypeStruct((16, ROWS), F32)],
            in_specs=[pl.BlockSpec(memory_space=pltpu.HBM)] * 8,
            out_specs=[pl.BlockSpec(memory_space=pltpu.VMEM)] * 4,
            scratch_shapes=[
                pltpu.VMEM((ROWS, COLS), BF16),
                pltpu.VMEM((ROWS, COLS), BF16),
                pltpu.VMEM((ROWS, COLS), BF16),
                pltpu.VMEM((16, ROWS), F32),
                pltpu.VMEM(wave.shape, BF16),
                pltpu.VMEM(twist.shape, F32),
                pltpu.VMEM(turned.shape, F32),
                pltpu.VMEM(small.shape, BF16),
                pltpu.VMEM((ROWS * 16, LANES), F32),
                pltpu.VMEM((8, ROWS, COLS), F32),
                pltpu.VMEM((WORKERS, 16, LANES), BF16),
                pltpu.VMEM((ROWS, 16, LANES), BF16),
                pltpu.VMEM((8, LANES), BF16),
                message,
                pltpu.VMEM((ROWS, 16, LANES), BF16),
                pltpu.VMEM((WORKERS, 16, LANES), BF16),
                message,
                message,
                pltpu.VMEM((8, LANES), BF16),
                pltpu.VMEM((8, 8, LANES), BF16),
                pltpu.SemaphoreType.DMA((4,)),
                pltpu.SemaphoreType.DMA((4,)),
                pltpu.SemaphoreType.DMA((6,)),
                pltpu.SemaphoreType.DMA((6,)),
                pltpu.SemaphoreType.REGULAR,
            ],
            compiler_params=pltpu.CompilerParams(
                collective_id=0, has_side_effects=True, vmem_limit_bytes=40 * 1024 * 1024
            ),
        )(
            *hbm(pregate.reshape(ROWS, COLS),
            gate.reshape(ROWS, COLS),
            upstream.reshape(ROWS, COLS),
            filter_taps.T,
            jnp.asarray(wave),
            jnp.asarray(twist),
            jnp.asarray(turned),
            jnp.asarray(small)),
        )
        results = pl.pallas_call(
            hand_over,
            out_shape=[block, block, block, jax.ShapeDtypeStruct((16, ROWS), F32)],
            in_specs=[pl.BlockSpec(memory_space=pl.ANY)] * 4,
            out_specs=[pl.BlockSpec(memory_space=pl.ANY)] * 4,
            scratch_shapes=[pltpu.SemaphoreType.DMA((4,))],
            compiler_params=pltpu.CompilerParams(vmem_limit_bytes=40 * 1024 * 1024),
        )(*results)
        shape = pregate.shape
        return tuple(value.reshape(shape) for value in results[:3]) + (results[3].T,)

    whole = P("dp", "tensor", "context")
    specs = (whole, whole, whole, P(None, "context"))
    return jax.shard_map(body, mesh=mesh, in_specs=specs, out_specs=specs, check_vma=False)
```

```python
import math

import jax
import jax.numpy as jnp
import ml_dtypes
import numpy as np
from jax import lax
from jax.experimental import pallas as pl
from jax.experimental.pallas import tpu as pltpu
from jax.sharding import PartitionSpec as P


COLS = 512
ROWS = 32
POINTS = ROWS * COLS
LANES = 128
QUADS = COLS // LANES
SLABS = 8
COPIES = 2 * SLABS
WORKERS = 16
F32 = jnp.float32
BF16 = jnp.bfloat16
MESH = pl.DeviceIdType.MESH


def split(table):
    high = table.astype(ml_dtypes.bfloat16)
    low = (table - high.astype(np.float64)).astype(ml_dtypes.bfloat16)
    return high, low


def make_tables(norm):
    r = np.arange(ROWS)
    k1 = np.arange(ROWS)
    c = np.arange(COLS)
    inner = 2.0 * np.pi * (np.outer(c, c) % COLS) / COLS
    wave = np.concatenate([np.cos(inner), np.sin(inner)], axis=1)
    wave = np.concatenate(split(wave), axis=0)
    wave = np.stack(np.split(wave, 2 * QUADS, axis=1))
    phase = 2.0 * np.pi * (np.outer(4 * k1 + 1, c) % (4 * POINTS)) / (4 * POINTS)
    twist = np.stack([np.cos(phase), np.sin(phase)]).astype(np.float32)
    turned = np.concatenate([np.cos(phase.T)] * 2 + [np.sin(phase.T)] * 2, axis=1).astype(np.float32)
    outer = 2.0 * np.pi * (np.outer(4 * k1 + 1, r) % (4 * ROWS)) / (4 * ROWS)
    first = np.concatenate([np.cos(outer), -np.sin(outer)], axis=0)
    first_high, first_low = split(first)
    analyse = np.concatenate([first_high, first_low], axis=1)
    analyse_taps = np.concatenate(
        [np.concatenate([first_high] * 4, axis=1), np.concatenate([first_low] * 4, axis=1)], axis=0
    )
    last_high, last_low = split(first.T / POINTS)
    build = np.concatenate([last_high, last_low], axis=1)
    wide = np.concatenate([first * (norm / POINTS)] * 2, axis=0)
    wide = np.concatenate([wide] * 4, axis=1)
    build_taps = np.concatenate(split(wide), axis=0)
    small = np.zeros((5, 256, LANES), ml_dtypes.bfloat16)
    small[0, :64, :64] = analyse
    small[1, :128] = analyse_taps
    small[2, :32] = build
    small[3, :256] = build_taps
    return wave, twist, turned, small[:4]


def mm(a, b):
    return jnp.dot(a, b, preferred_element_type=F32)


def mm_nt(a, b):
    return lax.dot_general(a, b, (((1,), (1,)), ((), ())), preferred_element_type=F32)


def pair(value):
    lane = lax.broadcasted_iota(jnp.int32, value.shape, value.ndim - 1)
    high = value.astype(BF16).astype(F32)
    return jnp.where(lax.rem(lane, 64) < 32, high, value - high).astype(BF16)


def kernel(
    pre_hbm, gate_hbm, up_hbm, taps_hbm, wave_hbm, twist_hbm, turned_hbm, small_hbm,
    out_ref, gg_ref, gp_ref, gf_ref,
    pre_v, gate_v, up_v, taps_v, wave_v, twist_v, turned_v, small_v, pack_v, rough_v, half_v,
    main_s, main_r, taps_s, taps_r, back_s, back_r, part_s, part_r, sum_s, sum_r,
    in_sem, table_sem, send_sem, recv_sem, ready_sem,
):
    dp = lax.axis_index("dp")
    tensor = lax.axis_index("tensor")
    me = lax.axis_index("context")
    x, z = me // SLABS, lax.rem(me, SLABS)
    plane = x * SLABS + tensor
    side = z // 4
    worker = (z >= 2) & (z < 6)
    idle = (z < 2) | (z >= 6)
    mine = x * 4 + z - 2

    def row_peer(step):
        mirrored = z + side * (7 - 2 * z)
        far = 7 - step // 4
        far = far - (mirrored - far + 8) // 8
        far = far + step // 28 * (mirrored - far)
        return (dp, tensor, lax.rem(x + 3 - lax.rem(step, 4), 4) * SLABS + far + side * (7 - 2 * far))

    def worker_place(step):
        far = 5 - step // 4
        return lax.rem(x + 3 - lax.rem(step, 4), 4), far + side * (7 - 2 * far)

    def worker_peer(step):
        wx, wz = worker_place(step)
        return (dp, tensor, wx * SLABS + wz)

    def tensor_peer(step):
        return (dp, lax.rem(tensor + step, SLABS), me)

    def plane_place(step):
        return lax.rem(x + 3 - lax.rem(step, 4), 4), step // 4

    def owner(step):
        return (1 - dp, lax.rem(tensor + 1 + step, SLABS), plane)

    def near_owner(step):
        return (dp, lax.rem(tensor + step, SLABS), plane)

    def sum_peer(step):
        return (1 - dp, z, x * SLABS + 2 + step)

    barrier = pltpu.get_barrier_semaphore()

    def greet(peers, start, stop):
        def signal(step, carry):
            pl.semaphore_signal(barrier, inc=1, device_id=peers(step), device_id_type=MESH)
            return carry

        lax.fori_loop(start, stop, signal, 0)

    @pl.when(dp == 0)
    def _():
        greet(sum_peer, 0, 4)

        @pl.when(worker)
        def _():
            greet(owner, 0, SLABS)

    @pl.when(worker)
    def _():
        greet(row_peer, 0, ROWS - 1)

    @pl.when(idle)
    def _():
        greet(worker_peer, 0, WORKERS)

    greet(tensor_peer, 1, SLABS)

    loads = [
        pltpu.make_async_copy(src, dst, in_sem.at[n])
        for n, (src, dst) in enumerate(
            [(pre_hbm, pre_v), (gate_hbm, gate_v), (up_hbm, up_v), (taps_hbm, taps_v)]
        )
    ]
    tables = [
        pltpu.make_async_copy(src, dst, table_sem.at[n])
        for n, (src, dst) in enumerate(
            [(small_hbm, small_v), (twist_hbm, twist_v), (wave_hbm, wave_v), (turned_hbm, turned_v)]
        )
    ]
    for copy in loads:
        copy.start()
    for copy in tables:
        copy.start()
    for copy in loads:
        copy.wait()

    gate = gate_v[...].astype(F32)
    up = up_v[...].astype(F32)
    dconv = (up * gate).astype(BF16).astype(F32)
    pre = pre_v[...].astype(F32)
    for p, signal in enumerate((pre, dconv)):
        for q in range(QUADS):
            pack_v[pl.ds(p * QUADS + q, ROWS, stride=8), :] = signal[:, q * LANES:(q + 1) * LANES]
    main_s[...] = pack_v[:ROWS * 8].reshape(WORKERS, 16, LANES).astype(BF16)

    taps = taps_v[...]
    taps_high = taps.astype(BF16).astype(F32)
    taps_low = taps - taps_high
    taps_s[...] = jnp.concatenate(
        [taps_high[:8], taps_low[:8], taps_high[8:], taps_low[8:]], axis=1
    ).astype(BF16)

    for condition, count in (
        (worker & (dp == 0), ROWS - 1 + SLABS - 1),
        (idle & (dp == 0), WORKERS + SLABS - 1),
        (worker & (dp == 1), ROWS - 1 + SLABS - 1 + SLABS + 4),
        (idle & (dp == 1), WORKERS + SLABS - 1 + 4),
    ):
        @pl.when(condition)
        def _(count=count):
            pl.semaphore_wait(barrier, count)

    def send(source, target, phase, peer, slot):
        pltpu.make_async_remote_copy(
            src_ref=source,
            dst_ref=target.at[slot],
            send_sem=send_sem.at[phase],
            recv_sem=recv_sem.at[phase],
            device_id=peer,
            device_id_type=MESH,
        ).start()

    def exchange(source, target, phase, peers, start, stop, slot):
        def one(step, carry):
            send(source(step), target, phase, peers(step), slot)
            return carry

        lax.fori_loop(start, stop, one, 0)

    def keep(source, target, phase, slot):
        pltpu.make_async_copy(source, target.at[slot], recv_sem.at[phase]).start()

    def arrive(target, phase):
        pltpu.make_async_copy(target, target, recv_sem.at[phase]).wait()

    def left(target, phase, count):
        part = target.at[pl.ds(0, count)]
        pltpu.make_async_copy(part, part, send_sem.at[phase]).wait()

    def to_workers(source, target, phase):
        def one(step, carry):
            wx, wz = worker_place(step)

            @pl.when((wx != x) | (wz != z))
            def _():
                send(source(wx * 4 + wz - 2), target, phase, worker_peer(step), me)

            return carry

        lax.fori_loop(0, WORKERS, one, 0)

    block = z * 4 + x
    first = lax.rem(tensor - z + SLABS, SLABS)
    own_taps = worker & (lax.rem(mine + SLABS, SLABS) == first)
    for w in (first, first + SLABS):
        @pl.when((w != mine) | idle)
        def _(w=w):
            send(taps_s, taps_r, 1, (dp, tensor, w // 4 * SLABS + 2 + lax.rem(w, 4)), block)

    to_workers(lambda w: main_s.at[w], main_r, 0)

    @pl.when(dp == 1)
    def _():
        def signal(step, carry):
            pl.semaphore_signal(ready_sem, inc=1, device_id=sum_peer(step), device_id_type=MESH)
            return carry

        lax.fori_loop(0, 4, signal, 0)

    for copy in tables:
        copy.wait()

    @pl.when(worker)
    def _():
        keep(main_s.at[mine], main_r, 0, me)
        slab = lax.rem(tensor + COPIES - mine, SLABS)
        held = taps_r.at[pl.ds(slab * 4, 4)]

        @pl.when(own_taps)
        def _():
            keep(taps_s, taps_r, 1, block)

        arrive(held, 1)
        exchange(lambda s: held, taps_r, 5, tensor_peer, 1, SLABS, pl.ds(slab * 4, 4))
        wave_high = jnp.concatenate([wave_v[n, :COLS] for n in range(2 * QUADS)], axis=1)
        wave_low = jnp.concatenate([wave_v[n, COLS:] for n in range(2 * QUADS)], axis=1)
        cos = twist_v[0]
        sin = twist_v[1]

        def forward_twist(re, im):
            return (re * cos + im * sin).astype(BF16), (im * cos - re * sin).astype(BF16)

        def inverse_twist(re, im):
            return (re * cos - im * sin).astype(BF16), (re * sin + im * cos).astype(BF16)

        arrive(main_r, 0)
        pack_v[...] = main_r[...].astype(F32).reshape(ROWS * 16, LANES)
        analyse = small_v[0, :64, :64]
        rows = [pack_v[pl.ds(n, ROWS, stride=16), :] for n in range(4 * QUADS)]
        grid = jnp.concatenate(rows, axis=1).astype(BF16)
        part = mm(analyse, jnp.concatenate([grid, grid], axis=0))
        halves = []
        for n in range(4):
            at = part[:, n * COLS:(n + 1) * COLS]
            halves.extend(forward_twist(at[:32], at[32:]))
        lhs = jnp.concatenate(halves, axis=0)
        half_v[...] = lhs
        rough = mm(lhs, wave_high)
        rough_v[...] = rough

        def spectrum(wide, base):
            re_c, re_s = wide[base:base + 32, :COLS], wide[base:base + 32, COLS:]
            im_c, im_s = wide[base + 32:base + 64, :COLS], wide[base + 32:base + 64, COLS:]
            return re_c + im_s, im_c - re_s

        specs = [spectrum(rough, 64 * n) for n in range(4)]

        x_re = x_im = 0.0
        for (pre_re, pre_im), (dc_re, dc_im) in (specs[:2], specs[2:]):
            x_re = x_re + pre_re * dc_re + pre_im * dc_im
            x_im = x_im + pre_re * dc_im - pre_im * dc_re
        x_re, x_im = x_re.astype(BF16), x_im.astype(BF16)
        up_row = jnp.concatenate([x_re, -x_im], axis=1)
        mid_row = jnp.concatenate([x_im, x_re], axis=1)
        low_row = jnp.concatenate([-x_im, -x_re], axis=1)
        rhs = jnp.concatenate([up_row, mid_row, low_row, up_row], axis=0)
        back = mm_nt(wave_high, rhs)
        back = (back * turned_v[...]).astype(BF16)
        share = mm(jnp.concatenate([back, back], axis=1), small_v[3])
        share = share.reshape(ROWS, 2, 8, LANES)
        lane = lax.broadcasted_iota(jnp.int32, (ROWS, 8, LANES), 2)
        share = jnp.where(lane < 64, share[:, 0], share[:, 1])
        part_s[...] = pair(share)

        def shares():

            def one(step, carry):
                px, pt = plane_place(step)

                @pl.when((px != x) | (pt != tensor))
                def _():
                    send(part_s.at[px * SLABS + pt], part_r, 2, (dp, pt, px * SLABS + z), plane)

                return carry

            lax.fori_loop(0, ROWS, one, 0)
            keep(part_s.at[plane], part_r, 2, plane)

        def convolutions():
            fine = rough_v[...] + mm(half_v[...], wave_low)
            specs = [spectrum(fine, 64 * n) for n in range(4)]
            lane = lax.broadcasted_iota(jnp.int32, (ROWS, 8, LANES), 2)
            arrive(taps_r.at[pl.ds(0, ROWS - 4)], 5)
            taps = taps_r[...].astype(F32).reshape(SLABS, 4, 8, LANES)
            taps = jnp.stack([taps[n % SLABS, n // SLABS] for n in range(ROWS)])
            taps = jnp.stack([jnp.where(lane < 64, taps, 0.0), jnp.where(lane < 64, 0.0, taps)], axis=1)
            taps = taps.reshape(COLS, LANES).astype(BF16)
            part = mm_nt(small_v[1, :64], taps) + mm_nt(small_v[1, 64:128], taps)
            lhs = jnp.concatenate(forward_twist(part[:32], part[32:]), axis=0)
            wide = mm(lhs, wave_high) + mm(lhs, wave_low)
            f_re, f_im = spectrum(wide, 0)

            products = []
            for (pre_re, pre_im), (dc_re, dc_im) in (specs[:2], specs[2:]):
                products += [
                    pre_re * f_re - pre_im * f_im,
                    pre_re * f_im + pre_im * f_re,
                    f_re * dc_re + f_im * dc_im,
                    f_re * dc_im - f_im * dc_re,
                ]
            lhs = jnp.concatenate([product.astype(BF16) for product in products], axis=0)
            wide = mm(lhs, wave_high) + mm(lhs, wave_low)
            build = small_v[2, :32]
            for n in range(4):
                base = 64 * n
                re_c, re_s = wide[base:base + 32, :COLS], wide[base:base + 32, COLS:]
                im_c, im_s = wide[base + 32:base + 64, :COLS], wide[base + 32:base + 64, COLS:]
                half = jnp.concatenate(inverse_twist(re_c - im_s, re_s + im_c), axis=0)
                result = mm(build, jnp.concatenate([half, half], axis=0))
                for q in range(QUADS):
                    pack_v[pl.ds(n * QUADS + q, ROWS, stride=16), :] = result[:, q * LANES:(q + 1) * LANES]
            back_s[...] = pack_v[...].reshape(ROWS, 16, LANES).astype(BF16)
            keep(back_s.at[me], back_r, 3, mine)
            exchange(lambda s: back_s.at[row_peer(s)[2]], back_r, 3, row_peer, 0, ROWS - 1, mine)

        def sums():
            arrive(part_r, 2)
            total = jnp.sum(part_r[...].astype(F32), axis=0)
            lane = lax.broadcasted_iota(jnp.int32, (8, LANES), 1)
            total = total + jnp.where(lax.rem(lane, 64) < 32, pltpu.roll(total, 96, 1), pltpu.roll(total, 32, 1))
            sum_s[...] = pair(total)
            spot = dp * 4 + z - 2

            @pl.when(dp == 1)
            def _():
                exchange(lambda s: sum_s, sum_r, 4, owner, 0, SLABS, spot)

            exchange(lambda s: sum_s, sum_r, 4, near_owner, 1, SLABS, spot)

            @pl.when(z == tensor)
            def _():
                keep(sum_s, sum_r, 4, spot)

            @pl.when(z != tensor)
            def _():
                send(sum_s, sum_r, 4, near_owner(0), spot)

            @pl.when(dp == 0)
            def _():
                pl.semaphore_wait(ready_sem, SLABS)
                exchange(lambda s: sum_s, sum_r, 4, owner, 0, SLABS, spot)

        @pl.when(dp == 0)
        def _():
            convolutions()
            shares()
            sums()

        @pl.when(dp == 1)
        def _():
            shares()
            sums()
            convolutions()

    arrive(back_r, 3)
    pack_v[:ROWS * 8] = back_r[...].astype(F32).reshape(ROWS * 8, LANES)
    rows = [pack_v[pl.ds(n, ROWS, stride=8), :] for n in range(8)]
    conv = jnp.concatenate(rows[:QUADS], axis=1)
    out_ref[...] = (gate * conv).astype(BF16)
    gg_ref[...] = (up * conv).astype(BF16)
    gp_ref[...] = jnp.concatenate(rows[QUADS:], axis=1).astype(BF16)

    arrive(sum_r, 4)
    total = jnp.sum(sum_r[...].astype(F32), axis=0)
    total = total + pltpu.roll(total, 96, 1)
    gf_ref[0:8, :] = total[:, 0:32]
    gf_ref[8:16, :] = total[:, 64:96]

    left(main_r, 0, WORKERS - 1)
    left(taps_r, 1, 1)

    @pl.when(idle)
    def _():
        left(main_r, 0, 1)

    @pl.when(jnp.logical_not(own_taps))
    def _():
        left(taps_r, 1, 1)

    @pl.when(worker)
    def _():
        left(taps_r, 5, ROWS - 4)
        left(part_r, 2, ROWS - 1)
        left(back_s, 3, ROWS - 1)
        left(part_r, 4, COPIES - 1)

        @pl.when(z != tensor)
        def _():
            left(part_r, 4, 1)


def hbm(*xs):
    return [pltpu.with_memory_space_constraint(x, pltpu.HBM) for x in xs]


def hand_over(a, b, c, d, a_out, b_out, c_out, d_out, sem):
    pairs = [(a, a_out), (b, b_out), (c, c_out), (d, d_out)]
    copies = [pltpu.make_async_copy(src, dst, sem.at[n]) for n, (src, dst) in enumerate(pairs)]
    for copy in copies:
        copy.start()
    for copy in copies:
        copy.wait()


def solution(mesh):
    norm = 1.0 / math.sqrt(mesh.size * POINTS)
    wave, twist, turned, small = make_tables(norm)

    def body(pregate, gate, upstream, filter_taps):
        block = jax.ShapeDtypeStruct((ROWS, COLS), BF16)
        message = pltpu.VMEM((ROWS, 8, LANES), BF16)
        results = pl.pallas_call(
            kernel,
            out_shape=[block, block, block, jax.ShapeDtypeStruct((16, ROWS), F32)],
            in_specs=[pl.BlockSpec(memory_space=pltpu.HBM)] * 8,
            out_specs=[pl.BlockSpec(memory_space=pltpu.VMEM)] * 4,
            scratch_shapes=[
                pltpu.VMEM((ROWS, COLS), BF16),
                pltpu.VMEM((ROWS, COLS), BF16),
                pltpu.VMEM((ROWS, COLS), BF16),
                pltpu.VMEM((16, ROWS), F32),
                pltpu.VMEM(wave.shape, BF16),
                pltpu.VMEM(twist.shape, F32),
                pltpu.VMEM(turned.shape, F32),
                pltpu.VMEM(small.shape, BF16),
                pltpu.VMEM((ROWS * 16, LANES), F32),
                pltpu.VMEM((256, 2 * COLS), F32),
                pltpu.VMEM((256, COLS), BF16),
                pltpu.VMEM((WORKERS, 16, LANES), BF16),
                pltpu.VMEM((ROWS, 16, LANES), BF16),
                pltpu.VMEM((8, LANES), BF16),
                message,
                pltpu.VMEM((ROWS, 16, LANES), BF16),
                pltpu.VMEM((WORKERS, 16, LANES), BF16),
                message,
                message,
                pltpu.VMEM((8, LANES), BF16),
                pltpu.VMEM((8, 8, LANES), BF16),
                pltpu.SemaphoreType.DMA((4,)),
                pltpu.SemaphoreType.DMA((4,)),
                pltpu.SemaphoreType.DMA((6,)),
                pltpu.SemaphoreType.DMA((6,)),
                pltpu.SemaphoreType.REGULAR,
            ],
            compiler_params=pltpu.CompilerParams(
                collective_id=0, has_side_effects=True, vmem_limit_bytes=40 * 1024 * 1024
            ),
        )(
            *hbm(pregate.reshape(ROWS, COLS),
            gate.reshape(ROWS, COLS),
            upstream.reshape(ROWS, COLS),
            filter_taps.T,
            jnp.asarray(wave),
            jnp.asarray(twist),
            jnp.asarray(turned),
            jnp.asarray(small)),
        )
        results = pl.pallas_call(
            hand_over,
            out_shape=[block, block, block, jax.ShapeDtypeStruct((16, ROWS), F32)],
            in_specs=[pl.BlockSpec(memory_space=pl.ANY)] * 4,
            out_specs=[pl.BlockSpec(memory_space=pl.ANY)] * 4,
            scratch_shapes=[pltpu.SemaphoreType.DMA((4,))],
            compiler_params=pltpu.CompilerParams(vmem_limit_bytes=40 * 1024 * 1024),
        )(*results)
        shape = pregate.shape
        return tuple(value.reshape(shape) for value in results[:3]) + (results[3].T,)

    whole = P("dp", "tensor", "context")
    specs = (whole, whole, whole, P(None, "context"))
    return jax.shard_map(body, mesh=mesh, in_specs=specs, out_specs=specs, check_vma=False)
```

```python
import math

import jax
import jax.numpy as jnp
import ml_dtypes
import numpy as np
from jax import lax
from jax.experimental import pallas as pl
from jax.experimental.pallas import tpu as pltpu
from jax.sharding import PartitionSpec as P


COLS = 512
ROWS = 32
POINTS = ROWS * COLS
LANES = 128
QUADS = COLS // LANES
SLABS = 8
COPIES = 2 * SLABS
WORKERS = 16
F32 = jnp.float32
BF16 = jnp.bfloat16
MESH = pl.DeviceIdType.MESH


def split(table):
    high = table.astype(ml_dtypes.bfloat16)
    low = (table - high.astype(np.float64)).astype(ml_dtypes.bfloat16)
    return high, low


def make_tables(norm):
    r = np.arange(ROWS)
    k1 = np.arange(ROWS)
    c = np.arange(COLS)
    inner = 2.0 * np.pi * (np.outer(c, c) % COLS) / COLS
    wave = np.concatenate([np.cos(inner), np.sin(inner)], axis=1)
    wave = np.concatenate(split(wave), axis=0)
    wave = np.stack(np.split(wave, 2 * QUADS, axis=1))
    phase = 2.0 * np.pi * (np.outer(4 * k1 + 1, c) % (4 * POINTS)) / (4 * POINTS)
    twist = np.stack([np.cos(phase), np.sin(phase)]).astype(np.float32)
    turned = np.concatenate([np.cos(phase.T)] * 2 + [np.sin(phase.T)] * 2, axis=1).astype(np.float32)
    outer = 2.0 * np.pi * (np.outer(4 * k1 + 1, r) % (4 * ROWS)) / (4 * ROWS)
    first = np.concatenate([np.cos(outer), -np.sin(outer)], axis=0)
    first_high, first_low = split(first)
    analyse = np.concatenate([first_high, first_low], axis=1)
    analyse_taps = np.concatenate(
        [np.concatenate([first_high] * 4, axis=1), np.concatenate([first_low] * 4, axis=1)], axis=0
    )
    last_high, last_low = split(first.T / POINTS)
    build = np.concatenate([last_high, last_low], axis=1)
    wide = np.concatenate([first * (norm / POINTS)] * 2, axis=0)
    wide = np.concatenate([wide] * 4, axis=1)
    build_taps = np.concatenate(split(wide), axis=0)
    small = np.zeros((5, 256, LANES), ml_dtypes.bfloat16)
    small[0, :64, :64] = analyse
    small[1, :128] = analyse_taps
    small[2, :32] = build
    small[3, :256] = build_taps
    return wave, twist, turned, small[:4]


def mm(a, b):
    return jnp.dot(a, b, preferred_element_type=F32)


def mm_nt(a, b):
    return lax.dot_general(a, b, (((1,), (1,)), ((), ())), preferred_element_type=F32)


def pair(value):
    lane = lax.broadcasted_iota(jnp.int32, value.shape, value.ndim - 1)
    high = value.astype(BF16).astype(F32)
    return jnp.where(lax.rem(lane, 64) < 32, high, value - high).astype(BF16)


def kernel(
    pre_hbm, gate_hbm, up_hbm, taps_hbm, wave_hbm, twist_hbm, turned_hbm, small_hbm,
    out_ref, gg_ref, gp_ref, gf_ref,
    pre_v, gate_v, up_v, taps_v, wave_v, twist_v, turned_v, small_v, pack_v, rough_v, half_v,
    main_s, main_r, taps_s, taps_r, back_s, back_r, part_s, part_r, sum_s, sum_r,
    in_sem, table_sem, send_sem, recv_sem, ready_sem,
):
    dp = lax.axis_index("dp")
    tensor = lax.axis_index("tensor")
    me = lax.axis_index("context")
    x, z = me // SLABS, lax.rem(me, SLABS)
    plane = x * SLABS + tensor
    side = z // 4
    worker = (z >= 2) & (z < 6)
    idle = (z < 2) | (z >= 6)
    mine = x * 4 + z - 2

    def row_peer(step):
        mirrored = z + side * (7 - 2 * z)
        far = 7 - step // 4
        far = far - (mirrored - far + 8) // 8
        far = far + step // 28 * (mirrored - far)
        return (dp, tensor, lax.rem(x + 3 - lax.rem(step, 4), 4) * SLABS + far + side * (7 - 2 * far))

    def worker_place(step):
        far = 5 - step // 4
        return lax.rem(x + 3 - lax.rem(step, 4), 4), far + side * (7 - 2 * far)

    def worker_peer(step):
        wx, wz = worker_place(step)
        return (dp, tensor, wx * SLABS + wz)

    def tensor_peer(step):
        return (dp, lax.rem(tensor + step, SLABS), me)

    def plane_place(step):
        return lax.rem(x + 3 - lax.rem(step, 4), 4), step // 4

    def owner(step):
        return (1 - dp, lax.rem(tensor + 1 + step, SLABS), plane)

    def near_owner(step):
        return (dp, lax.rem(tensor + step, SLABS), plane)

    def sum_peer(step):
        return (1 - dp, z, x * SLABS + 2 + step)

    barrier = pltpu.get_barrier_semaphore()

    def greet(peers, start, stop):
        def signal(step, carry):
            pl.semaphore_signal(barrier, inc=1, device_id=peers(step), device_id_type=MESH)
            return carry

        lax.fori_loop(start, stop, signal, 0)

    @pl.when(dp == 0)
    def _():
        greet(sum_peer, 0, 4)

        @pl.when(worker)
        def _():
            greet(owner, 0, SLABS)

    @pl.when(worker)
    def _():
        greet(row_peer, 0, ROWS - 1)

    @pl.when(idle)
    def _():
        greet(worker_peer, 0, WORKERS)

    greet(tensor_peer, 1, SLABS)

    loads = [
        pltpu.make_async_copy(src, dst, in_sem.at[n])
        for n, (src, dst) in enumerate(
            [(pre_hbm, pre_v), (gate_hbm, gate_v), (up_hbm, up_v), (taps_hbm, taps_v)]
        )
    ]
    tables = [
        pltpu.make_async_copy(src, dst, table_sem.at[n])
        for n, (src, dst) in enumerate(
            [(small_hbm, small_v), (twist_hbm, twist_v), (wave_hbm, wave_v), (turned_hbm, turned_v)]
        )
    ]
    for copy in loads:
        copy.start()
    for copy in tables:
        copy.start()
    for copy in loads:
        copy.wait()

    gate = gate_v[...].astype(F32)
    up = up_v[...].astype(F32)
    dconv = (up * gate).astype(BF16).astype(F32)
    pre = pre_v[...].astype(F32)
    for p, signal in enumerate((pre, dconv)):
        for q in range(QUADS):
            pack_v[pl.ds(p * QUADS + q, ROWS, stride=8), :] = signal[:, q * LANES:(q + 1) * LANES]
    main_s[...] = pack_v[:ROWS * 8].reshape(WORKERS, 16, LANES).astype(BF16)

    taps = taps_v[...]
    taps_high = taps.astype(BF16).astype(F32)
    taps_low = taps - taps_high
    taps_s[...] = jnp.concatenate(
        [taps_high[:8], taps_low[:8], taps_high[8:], taps_low[8:]], axis=1
    ).astype(BF16)

    for condition, count in (
        (worker & (dp == 0), ROWS - 1 + SLABS - 1),
        (idle & (dp == 0), WORKERS + SLABS - 1),
        (worker & (dp == 1), ROWS - 1 + SLABS - 1 + SLABS + 4),
        (idle & (dp == 1), WORKERS + SLABS - 1 + 4),
    ):
        @pl.when(condition)
        def _(count=count):
            pl.semaphore_wait(barrier, count)

    def send(source, target, phase, peer, slot):
        pltpu.make_async_remote_copy(
            src_ref=source,
            dst_ref=target.at[slot],
            send_sem=send_sem.at[phase],
            recv_sem=recv_sem.at[phase],
            device_id=peer,
            device_id_type=MESH,
        ).start()

    def exchange(source, target, phase, peers, start, stop, slot):
        def one(step, carry):
            send(source(step), target, phase, peers(step), slot)
            return carry

        lax.fori_loop(start, stop, one, 0)

    def keep(source, target, phase, slot):
        pltpu.make_async_copy(source, target.at[slot], recv_sem.at[phase]).start()

    def arrive(target, phase):
        pltpu.make_async_copy(target, target, recv_sem.at[phase]).wait()

    def left(target, phase, count):
        part = target.at[pl.ds(0, count)]
        pltpu.make_async_copy(part, part, send_sem.at[phase]).wait()

    def to_workers(source, target, phase):
        def one(step, carry):
            wx, wz = worker_place(step)

            @pl.when((wx != x) | (wz != z))
            def _():
                send(source(wx * 4 + wz - 2), target, phase, worker_peer(step), me)

            return carry

        lax.fori_loop(0, WORKERS, one, 0)

    block = z * 4 + x
    first = lax.rem(tensor - z + SLABS, SLABS)
    own_taps = worker & (lax.rem(mine + SLABS, SLABS) == first)
    for w in (first, first + SLABS):
        @pl.when((w != mine) | idle)
        def _(w=w):
            send(taps_s, taps_r, 1, (dp, tensor, w // 4 * SLABS + 2 + lax.rem(w, 4)), block)

    to_workers(lambda w: main_s.at[w], main_r, 0)

    @pl.when(dp == 1)
    def _():
        def signal(step, carry):
            pl.semaphore_signal(ready_sem, inc=1, device_id=sum_peer(step), device_id_type=MESH)
            return carry

        lax.fori_loop(0, 4, signal, 0)

    for copy in tables:
        copy.wait()

    @pl.when(worker)
    def _():
        keep(main_s.at[mine], main_r, 0, me)
        slab = lax.rem(tensor + COPIES - mine, SLABS)
        held = taps_r.at[pl.ds(slab * 4, 4)]

        @pl.when(own_taps)
        def _():
            keep(taps_s, taps_r, 1, block)

        arrive(held, 1)
        exchange(lambda s: held, taps_r, 5, tensor_peer, 1, SLABS, pl.ds(slab * 4, 4))
        wave_high = jnp.concatenate([wave_v[n, :COLS] for n in range(2 * QUADS)], axis=1)
        wave_low = jnp.concatenate([wave_v[n, COLS:] for n in range(2 * QUADS)], axis=1)
        cos = twist_v[0]
        sin = twist_v[1]

        def forward_twist(re, im):
            return (re * cos + im * sin).astype(BF16), (im * cos - re * sin).astype(BF16)

        def inverse_twist(re, im):
            return (re * cos - im * sin).astype(BF16), (re * sin + im * cos).astype(BF16)

        arrive(main_r, 0)
        pack_v[...] = main_r[...].astype(F32).reshape(ROWS * 16, LANES)
        analyse = small_v[0, :64, :64]
        rows = [pack_v[pl.ds(n, ROWS, stride=16), :] for n in range(4 * QUADS)]
        grid = jnp.concatenate(rows, axis=1).astype(BF16)
        part = mm(analyse, jnp.concatenate([grid, grid], axis=0))
        halves = []
        for n in range(4):
            at = part[:, n * COLS:(n + 1) * COLS]
            halves.extend(forward_twist(at[:32], at[32:]))
        lhs = jnp.concatenate(halves, axis=0)
        half_v[...] = lhs
        rough = mm(lhs, wave_high)
        rough_v[...] = rough

        def spectrum(wide, base):
            re_c, re_s = wide[base:base + 32, :COLS], wide[base:base + 32, COLS:]
            im_c, im_s = wide[base + 32:base + 64, :COLS], wide[base + 32:base + 64, COLS:]
            return re_c + im_s, im_c - re_s

        specs = [spectrum(rough, 64 * n) for n in range(4)]

        x_re = x_im = 0.0
        for (pre_re, pre_im), (dc_re, dc_im) in (specs[:2], specs[2:]):
            x_re = x_re + pre_re * dc_re + pre_im * dc_im
            x_im = x_im + pre_re * dc_im - pre_im * dc_re
        x_re, x_im = x_re.astype(BF16), x_im.astype(BF16)
        up_row = jnp.concatenate([x_re, -x_im], axis=1)
        mid_row = jnp.concatenate([x_im, x_re], axis=1)
        low_row = jnp.concatenate([-x_im, -x_re], axis=1)
        rhs = jnp.concatenate([up_row, mid_row, low_row, up_row], axis=0)
        back = mm_nt(wave_high, rhs)
        back = (back * turned_v[...]).astype(BF16)
        share = mm(jnp.concatenate([back, back], axis=1), small_v[3])
        share = share.reshape(ROWS, 2, 8, LANES)
        lane = lax.broadcasted_iota(jnp.int32, (ROWS, 8, LANES), 2)
        share = jnp.where(lane < 64, share[:, 0], share[:, 1])
        part_s[...] = pair(share)

        def shares():

            def one(step, carry):
                px, pt = plane_place(step)

                @pl.when((px != x) | (pt != tensor))
                def _():
                    send(part_s.at[px * SLABS + pt], part_r, 2, (dp, pt, px * SLABS + z), plane)

                return carry

            lax.fori_loop(0, ROWS, one, 0)
            keep(part_s.at[plane], part_r, 2, plane)

        def convolutions():
            fine = rough_v[...] + mm(half_v[...], wave_low)
            specs = [spectrum(fine, 64 * n) for n in range(4)]
            lane = lax.broadcasted_iota(jnp.int32, (ROWS, 8, LANES), 2)
            arrive(taps_r.at[pl.ds(0, ROWS - 4)], 5)
            taps = taps_r[...].astype(F32).reshape(SLABS, 4, 8, LANES)
            taps = jnp.stack([taps[n % SLABS, n // SLABS] for n in range(ROWS)])
            taps = jnp.stack([jnp.where(lane < 64, taps, 0.0), jnp.where(lane < 64, 0.0, taps)], axis=1)
            taps = taps.reshape(COLS, LANES).astype(BF16)
            part = mm_nt(small_v[1, :64], taps) + mm_nt(small_v[1, 64:128], taps)
            lhs = jnp.concatenate(forward_twist(part[:32], part[32:]), axis=0)
            wide = mm(lhs, wave_high) + mm(lhs, wave_low)
            f_re, f_im = spectrum(wide, 0)

            products = []
            for (pre_re, pre_im), (dc_re, dc_im) in (specs[:2], specs[2:]):
                products += [
                    pre_re * f_re - pre_im * f_im,
                    pre_re * f_im + pre_im * f_re,
                    f_re * dc_re + f_im * dc_im,
                    f_re * dc_im - f_im * dc_re,
                ]
            lhs = jnp.concatenate([product.astype(BF16) for product in products], axis=0)
            wide = mm(lhs, wave_high) + mm(lhs, wave_low)
            build = small_v[2, :32]
            for n in range(4):
                base = 64 * n
                re_c, re_s = wide[base:base + 32, :COLS], wide[base:base + 32, COLS:]
                im_c, im_s = wide[base + 32:base + 64, :COLS], wide[base + 32:base + 64, COLS:]
                half = jnp.concatenate(inverse_twist(re_c - im_s, re_s + im_c), axis=0)
                result = mm(build, jnp.concatenate([half, half], axis=0))
                for q in range(QUADS):
                    pack_v[pl.ds(n * QUADS + q, ROWS, stride=16), :] = result[:, q * LANES:(q + 1) * LANES]
            back_s[...] = pack_v[...].reshape(ROWS, 16, LANES).astype(BF16)
            keep(back_s.at[me], back_r, 3, mine)
            exchange(lambda s: back_s.at[row_peer(s)[2]], back_r, 3, row_peer, 0, ROWS - 1, mine)

        def sums():
            arrive(part_r, 2)
            total = jnp.sum(part_r[...].astype(F32), axis=0)
            lane = lax.broadcasted_iota(jnp.int32, (8, LANES), 1)
            total = total + jnp.where(lax.rem(lane, 64) < 32, pltpu.roll(total, 96, 1), pltpu.roll(total, 32, 1))
            sum_s[...] = pair(total)
            spot = dp * 4 + z - 2

            @pl.when(dp == 1)
            def _():
                exchange(lambda s: sum_s, sum_r, 4, owner, 0, SLABS, spot)

            exchange(lambda s: sum_s, sum_r, 4, near_owner, 1, SLABS, spot)

            @pl.when(z == tensor)
            def _():
                keep(sum_s, sum_r, 4, spot)

            @pl.when(z != tensor)
            def _():
                send(sum_s, sum_r, 4, near_owner(0), spot)

            @pl.when(dp == 0)
            def _():
                pl.semaphore_wait(ready_sem, SLABS)
                exchange(lambda s: sum_s, sum_r, 4, owner, 0, SLABS, spot)

        @pl.when(dp == 0)
        def _():
            shares()
            convolutions()
            sums()

        @pl.when(dp == 1)
        def _():
            shares()
            sums()
            convolutions()

    arrive(back_r, 3)
    pack_v[:ROWS * 8] = back_r[...].astype(F32).reshape(ROWS * 8, LANES)
    rows = [pack_v[pl.ds(n, ROWS, stride=8), :] for n in range(8)]
    conv = jnp.concatenate(rows[:QUADS], axis=1)
    out_ref[...] = (gate * conv).astype(BF16)
    gg_ref[...] = (up * conv).astype(BF16)
    gp_ref[...] = jnp.concatenate(rows[QUADS:], axis=1).astype(BF16)

    arrive(sum_r, 4)
    total = jnp.sum(sum_r[...].astype(F32), axis=0)
    total = total + pltpu.roll(total, 96, 1)
    gf_ref[0:8, :] = total[:, 0:32]
    gf_ref[8:16, :] = total[:, 64:96]

    left(main_r, 0, WORKERS - 1)
    left(taps_r, 1, 1)

    @pl.when(idle)
    def _():
        left(main_r, 0, 1)

    @pl.when(jnp.logical_not(own_taps))
    def _():
        left(taps_r, 1, 1)

    @pl.when(worker)
    def _():
        left(taps_r, 5, ROWS - 4)
        left(part_r, 2, ROWS - 1)
        left(back_s, 3, ROWS - 1)
        left(part_r, 4, COPIES - 1)

        @pl.when(z != tensor)
        def _():
            left(part_r, 4, 1)


def hbm(*xs):
    return [pltpu.with_memory_space_constraint(x, pltpu.HBM) for x in xs]


def hand_over(a, b, c, d, a_out, b_out, c_out, d_out, sem):
    pairs = [(a, a_out), (b, b_out), (c, c_out), (d, d_out)]
    copies = [pltpu.make_async_copy(src, dst, sem.at[n]) for n, (src, dst) in enumerate(pairs)]
    for copy in copies:
        copy.start()
    for copy in copies:
        copy.wait()


def solution(mesh):
    norm = 1.0 / math.sqrt(mesh.size * POINTS)
    wave, twist, turned, small = make_tables(norm)

    def body(pregate, gate, upstream, filter_taps):
        block = jax.ShapeDtypeStruct((ROWS, COLS), BF16)
        message = pltpu.VMEM((ROWS, 8, LANES), BF16)
        results = pl.pallas_call(
            kernel,
            out_shape=[block, block, block, jax.ShapeDtypeStruct((16, ROWS), F32)],
            in_specs=[pl.BlockSpec(memory_space=pltpu.HBM)] * 8,
            out_specs=[pl.BlockSpec(memory_space=pltpu.VMEM)] * 4,
            scratch_shapes=[
                pltpu.VMEM((ROWS, COLS), BF16),
                pltpu.VMEM((ROWS, COLS), BF16),
                pltpu.VMEM((ROWS, COLS), BF16),
                pltpu.VMEM((16, ROWS), F32),
                pltpu.VMEM(wave.shape, BF16),
                pltpu.VMEM(twist.shape, F32),
                pltpu.VMEM(turned.shape, F32),
                pltpu.VMEM(small.shape, BF16),
                pltpu.VMEM((ROWS * 16, LANES), F32),
                pltpu.VMEM((256, 2 * COLS), F32),
                pltpu.VMEM((256, COLS), BF16),
                pltpu.VMEM((WORKERS, 16, LANES), BF16),
                pltpu.VMEM((ROWS, 16, LANES), BF16),
                pltpu.VMEM((8, LANES), BF16),
                message,
                pltpu.VMEM((ROWS, 16, LANES), BF16),
                pltpu.VMEM((WORKERS, 16, LANES), BF16),
                message,
                message,
                pltpu.VMEM((8, LANES), BF16),
                pltpu.VMEM((8, 8, LANES), BF16),
                pltpu.SemaphoreType.DMA((4,)),
                pltpu.SemaphoreType.DMA((4,)),
                pltpu.SemaphoreType.DMA((6,)),
                pltpu.SemaphoreType.DMA((6,)),
                pltpu.SemaphoreType.REGULAR,
            ],
            compiler_params=pltpu.CompilerParams(
                collective_id=0, has_side_effects=True, vmem_limit_bytes=40 * 1024 * 1024
            ),
        )(
            *hbm(pregate.reshape(ROWS, COLS),
            gate.reshape(ROWS, COLS),
            upstream.reshape(ROWS, COLS),
            filter_taps.T,
            jnp.asarray(wave),
            jnp.asarray(twist),
            jnp.asarray(turned),
            jnp.asarray(small)),
        )
        results = pl.pallas_call(
            hand_over,
            out_shape=[block, block, block, jax.ShapeDtypeStruct((16, ROWS), F32)],
            in_specs=[pl.BlockSpec(memory_space=pl.ANY)] * 4,
            out_specs=[pl.BlockSpec(memory_space=pl.ANY)] * 4,
            scratch_shapes=[pltpu.SemaphoreType.DMA((4,))],
            compiler_params=pltpu.CompilerParams(vmem_limit_bytes=40 * 1024 * 1024),
        )(*results)
        shape = pregate.shape
        return tuple(value.reshape(shape) for value in results[:3]) + (results[3].T,)

    whole = P("dp", "tensor", "context")
    specs = (whole, whole, whole, P(None, "context"))
    return jax.shard_map(body, mesh=mesh, in_specs=specs, out_specs=specs, check_vma=False)
```
